256 devices in a mesh: resp: 2 (over core), ctx: 32 (over z_lo, y, x), tp: 4 (over z_hi).
Axes of the slice: x: 4, y: 4, z: 8 (z_hi: 4, z_lo: 2; z = z_hi * 2 + z_lo), core: 2. Of those that a mesh axis runs over, the one named last changes fastest.
Arguments:
- q_prompt: bfloat16 [4096, 4096], P(('resp', 'ctx'), 'tp'), may hold values from -4.5 to 4.5
- k_prompt: bfloat16 [4096, 512], P(('resp', 'ctx'), 'tp'), may hold values from -4.5 to 4.5
- v_prompt: bfloat16 [4096, 512], P(('resp', 'ctx'), 'tp'), may hold values from -4.5 to 4.5
- doc_ids: int32 [4096], P(('resp', 'ctx')), may hold values from 0 to 3, never falling along the last dimension, each value on 1 to 2048 neighbouring positions
- q_resp: bfloat16 [2, 2048, 4096], P('resp', 'ctx', 'tp'), may hold values from -4.5 to 4.5
- k_resp: bfloat16 [2, 2048, 512], P('resp', 'ctx', 'tp'), may hold values from -4.5 to 4.5
- v_resp: bfloat16 [2, 2048, 512], P('resp', 'ctx', 'tp'), may hold values from -4.5 to 4.5
- resp_len: int32 [2], replicated, may hold values from 512 to 2048, as said below
- out_weight: bfloat16 [4096, 5120], P('tp'), may hold values from -0.09375 to 0.09375
- grad_prompt: bfloat16 [4096, 5120], P(('resp', 'ctx'), 'tp'), may hold values from -6 to 6
- grad_resp: bfloat16 [2, 2048, 5120], P('resp', 'ctx', 'tp'), may hold values from -6 to 6
Outputs:
- out_prompt: bfloat16 [4096, 5120], P(('resp', 'ctx'), 'tp')
- out_resp: bfloat16 [2, 2048, 5120], P('resp', 'ctx', 'tp')
- grad_q_prompt: bfloat16 [4096, 4096], P(('resp', 'ctx'), 'tp')
- grad_k_prompt: bfloat16 [4096, 512], P(('resp', 'ctx'), 'tp')
- grad_v_prompt: bfloat16 [4096, 512], P(('resp', 'ctx'), 'tp')
- grad_q_resp: bfloat16 [2, 2048, 4096], P('resp', 'ctx', 'tp')
- grad_k_resp: bfloat16 [2, 2048, 512], P('resp', 'ctx', 'tp')
- grad_v_resp: bfloat16 [2, 2048, 512], P('resp', 'ctx', 'tp')
The draws below stay inside these ranges and needn't reach their ends.
Inputs may be any that keep to these rules, and one draw needn't show every extreme that they name: `resp_len`: one of the two responses has all 2048 tokens live.
All inputs are finite; a program needn't handle non-finite values.
Results may differ from the reference program's by a relative error of at most 0.028.
Values may be sent and summed in bfloat16 or wider, within the bound.
No kernel may reach another device: no remote copies, remote signals or barrier semaphores. Data moves between devices by JAX's collectives and lax.ppermute only.
A program may use at most 128 MiB of HBM per device.

```python
import math
import jax
import jax.numpy as jnp
import numpy as np
from jax import lax

D = 5120
HQ = 32
HK = 4
DH = 128
PROMPT = 4096
RESPONSE = 2048


def shared_keys(key):
    return jnp.clip(jax.random.normal(key, (PROMPT, HK * DH), jnp.float32), -4.5, 4.5)


def draw_k_prompt(key, part):
    key_field = shared_keys(key)
    return key_field.astype(jnp.bfloat16)


def draw_q_prompt(key, part):
    key = jax.random.fold_in(key, 5)
    query_field = jnp.clip(jax.random.normal(key, (PROMPT, HQ * DH), jnp.float32), -4.5, 4.5)
    return query_field.astype(jnp.bfloat16)


def draw_q_resp(key, part):
    key = jax.random.fold_in(key, 7)
    query_field = jnp.clip(jax.random.normal(key, (2, RESPONSE, HQ * DH), jnp.float32), -4.5, 4.5)
    return query_field.astype(jnp.bfloat16)


def draw_resp_len(key, part):
    key = jax.random.fold_in(key, 9)
    first_key, second_key = jax.random.split(key)
    other = jax.random.randint(first_key, (), RESPONSE // 4, RESPONSE + 1, dtype=jnp.int32)
    flipped = jax.random.randint(second_key, (), 0, 2, dtype=jnp.int32)
    full_len = jnp.int32(RESPONSE)
    return jnp.where(flipped == 0, jnp.stack([full_len, other]), jnp.stack([other, full_len])).astype(jnp.int32)


def shard_levels(own_key, extent, cuts, smallest, top_value):
    gain = 1.0
    for dim, parts in cuts:
        draws = jax.random.uniform(jax.random.fold_in(jax.random.fold_in(own_key, 6), dim), (parts,), jnp.float32, smallest / len(cuts), top_value / len(cuts))
        gain = gain * jnp.repeat(jnp.exp(draws), extent[dim] // parts).reshape((-1,) + (1,) * (len(extent) - 1 - dim))
    return gain


def split_up(count, total, limit, skew):
    portions = [(1 << 20) // math.isqrt(standing ** skew) + 1 for standing in range(2, count + 1)]
    spare, counts = total - limit - (count - 1), [1] * (count - 1)
    while spare > 0:
        candidates = [i for i in range(count - 1) if counts[i] < limit]
        pool, remaining = sum([portions[i] for i in candidates]), spare
        for i in candidates:
            extra = min(limit - counts[i], max(1, remaining * portions[i] // pool), spare)
            counts[i] = counts[i] + extra
            spare = spare - extra
    return np.array([limit] + counts)


def ragged_sizes(own_key, count, total, reach, slope):
    if count == 2:
        one = jax.random.randint(own_key, (), max(1, total - reach), min(reach, total - 1) + 1)
        return jnp.stack([one, total - one])
    sizes = jnp.asarray(split_up(count, total, reach, slope), jnp.int32)
    couples = (count - 1) // 2
    donor, taker = sizes[1:1 + 2 * couples:2], sizes[2:2 + 2 * couples:2]
    margin = jnp.minimum(donor - 1, reach - taker)
    moved = jax.random.randint(jax.random.fold_in(own_key, 1), (couples,), 0, 1 << 20) % (margin + 1)
    sizes = sizes.at[1:1 + 2 * couples:2].set(donor - moved).at[2:2 + 2 * couples:2].set(taker + moved)
    return sizes[jax.random.permutation(jax.random.fold_in(own_key, 2), count)]


def normal_values(rng, shape, deviation, bound, shards=(), kind=jnp.bfloat16):
    values = jax.random.normal(rng, shape, jnp.float32) * deviation
    if len(shards) > 0:
        values = shard_levels(rng, shape, shards, -0.22, 0.18) * values
    return jnp.clip(values, min=-bound, max=bound).astype(kind)


def setup_inputs(seed: int = 0) -> dict:
    key_list = jax.random.split(jax.random.key(seed), 12)
    q_prompt = draw_q_prompt(jax.random.fold_in(key_list[11], 71), 0)
    k_prompt = draw_k_prompt(jax.random.fold_in(key_list[11], 71), 0)
    v_prompt = normal_values(key_list[2], (PROMPT, HK * DH), 1.0, 4.5, ((0, 64), (1, 4)))
    doc_ids = jnp.searchsorted(jnp.cumsum(ragged_sizes(key_list[3], 4, PROMPT, PROMPT // 2, 0)), jnp.arange(PROMPT), side="right").astype(jnp.int32)
    q_resp = draw_q_resp(jax.random.fold_in(key_list[11], 71), 0)
    k_resp = normal_values(key_list[5], (2, RESPONSE, HK * DH), 1.0, 4.5, ((0, 2), (1, 32), (2, 4)))
    v_resp = normal_values(key_list[6], (2, RESPONSE, HK * DH), 1.0, 4.5, ((0, 2), (1, 32), (2, 4)))
    resp_len = draw_resp_len(jax.random.fold_in(key_list[11], 71), 0)
    out_weight = normal_values(key_list[8], (HQ * DH, D), (HQ * DH) ** -0.5, 0.09375, ((0, 4),))
    grad_prompt = normal_values(key_list[9], (PROMPT, D), 1.0, 6.0, ((0, 64), (1, 4)))
    grad_resp = normal_values(key_list[10], (2, RESPONSE, D), 1.0, 6.0, ((0, 2), (1, 32), (2, 4)))
    return {"q_prompt": q_prompt, "k_prompt": k_prompt, "v_prompt": v_prompt, "doc_ids": doc_ids, "q_resp": q_resp, "k_resp": k_resp, "v_resp": v_resp, "resp_len": resp_len, "out_weight": out_weight, "grad_prompt": grad_prompt, "grad_resp": grad_resp}


NEGATIVE = -1e+30

def attend_block(queries, keys, values, d_attended, visible):
    score_scale = 1.0 / math.sqrt(DH)
    scores = jnp.dot(queries, keys.T, preferred_element_type=jnp.float32) * score_scale
    top = lax.optimization_barrier(jnp.max(jnp.where(visible, scores, NEGATIVE), axis=1, keepdims=True))
    weights = jnp.where(visible, jnp.exp(scores - top), 0.0)
    total = lax.optimization_barrier(jnp.sum(weights, axis=1, keepdims=True))
    attended = (jnp.dot(weights.astype(jnp.bfloat16), values, preferred_element_type=jnp.float32) / total).astype(jnp.bfloat16)
    log_total = top + jnp.log(total)
    probs = jnp.where(visible, jnp.exp(scores - log_total), 0.0)
    grad_values = jnp.dot(probs.astype(jnp.bfloat16).T, d_attended, preferred_element_type=jnp.float32)
    dprobs = jnp.dot(d_attended, values.T, preferred_element_type=jnp.float32)
    row_delta = lax.optimization_barrier(jnp.sum(d_attended.astype(jnp.float32) * attended.astype(jnp.float32), axis=1, keepdims=True))
    score_grad = (probs * (dprobs - row_delta)).astype(jnp.bfloat16)
    grad_queries = score_scale * jnp.dot(score_grad, keys, preferred_element_type=jnp.float32)
    grad_keys = score_scale * jnp.dot(score_grad.T, queries, preferred_element_type=jnp.float32)
    return (attended, grad_queries, grad_keys, grad_values)

def reference(q_prompt, k_prompt, v_prompt, doc_ids, q_resp, k_resp, v_resp, resp_len, out_weight, grad_prompt, grad_resp):
    group_size = HQ // HK
    d_prompt = jnp.dot(grad_prompt, out_weight.T, preferred_element_type=jnp.float32).astype(jnp.bfloat16)
    d_resp = jnp.dot(grad_resp.reshape(2 * RESPONSE, D), out_weight.T, preferred_element_type=jnp.float32).astype(jnp.bfloat16)
    positions = jnp.arange(PROMPT, dtype=jnp.int32)
    prompt_visible = (positions[None, :] <= positions[:, None]) & (doc_ids[None, :] == doc_ids[:, None])
    resp_positions = jnp.arange(RESPONSE, dtype=jnp.int32)
    resp_visible = []
    for side in range(2):
        own_keys = (resp_positions[None, :] <= resp_positions[:, None]) & (resp_positions[None, :] < resp_len[side])
        resp_visible.append(jnp.concatenate([jnp.ones((RESPONSE, PROMPT), bool), own_keys], axis=1))

    def heads_first(array, rows, heads):
        return array.reshape(rows, heads, DH).transpose(1, 0, 2)
    q_heads = heads_first(q_prompt, PROMPT, HQ)
    k_heads = jnp.repeat(heads_first(k_prompt, PROMPT, HK), group_size, axis=0)
    v_heads = jnp.repeat(heads_first(v_prompt, PROMPT, HK), group_size, axis=0)
    dp_heads = heads_first(d_prompt, PROMPT, HQ)
    qr_heads = q_resp.reshape(2, RESPONSE, HQ, DH).transpose(2, 0, 1, 3)
    kr_heads = jnp.repeat(k_resp.reshape(2, RESPONSE, HK, DH).transpose(2, 0, 1, 3), group_size, axis=0)
    vr_heads = jnp.repeat(v_resp.reshape(2, RESPONSE, HK, DH).transpose(2, 0, 1, 3), group_size, axis=0)
    dr_heads = d_resp.reshape(2, RESPONSE, HQ, DH).transpose(2, 0, 1, 3)

    def one_head(block_item):
        qp_one, kp_one, vp_one, dp_one, qr_one, kr_one, vr_one, dr_one = block_item
        attended_p, gq_p, gk_p, gv_p = attend_block(qp_one, kp_one, vp_one, dp_one, prompt_visible)
        attended_r, gq_r, gk_r, gv_r = ([], [], [], [])
        for side in range(2):
            keys = jnp.concatenate([kp_one, kr_one[side]], axis=0)
            values = jnp.concatenate([vp_one, vr_one[side]], axis=0)
            outcome = attend_block(qr_one[side], keys, values, dr_one[side], resp_visible[side])
            attended_r.append(outcome[0])
            gq_r.append(outcome[1])
            gk_p = gk_p + outcome[2][:PROMPT]
            gv_p = gv_p + outcome[3][:PROMPT]
            gk_r.append(outcome[2][PROMPT:])
            gv_r.append(outcome[3][PROMPT:])
        return (attended_p, gq_p, gk_p, gv_p, jnp.stack(attended_r), jnp.stack(gq_r), jnp.stack(gk_r), jnp.stack(gv_r))
    results = lax.map(one_head, (q_heads, k_heads, v_heads, dp_heads, qr_heads, kr_heads, vr_heads, dr_heads))
    attended_p = results[0].transpose(1, 0, 2).reshape(PROMPT, HQ * DH)
    out_prompt = jnp.dot(attended_p, out_weight, preferred_element_type=jnp.float32).astype(jnp.bfloat16)
    attended_r = results[4].transpose(1, 2, 0, 3).reshape(2 * RESPONSE, HQ * DH)
    out_resp = jnp.dot(attended_r, out_weight, preferred_element_type=jnp.float32).astype(jnp.bfloat16).reshape(2, RESPONSE, D)
    grad_q_prompt = results[1].transpose(1, 0, 2).reshape(PROMPT, HQ * DH).astype(jnp.bfloat16)

    def kv_prompt(array):
        return array.reshape(HK, group_size, PROMPT, DH).sum(axis=1).transpose(1, 0, 2).reshape(PROMPT, HK * DH).astype(jnp.bfloat16)

    def kv_resp(array):
        return array.reshape(HK, group_size, 2, RESPONSE, DH).sum(axis=1).transpose(1, 2, 0, 3).reshape(2, RESPONSE, HK * DH).astype(jnp.bfloat16)
    grad_q_resp = results[5].transpose(1, 2, 0, 3).reshape(2, RESPONSE, HQ * DH).astype(jnp.bfloat16)
    return (out_prompt, out_resp, grad_q_prompt, kv_prompt(results[2]), kv_prompt(results[3]), grad_q_resp, kv_resp(results[6]), kv_resp(results[7]))
```

```python
import math

import jax
import jax.numpy as jnp
from jax import lax
from jax.experimental import pallas as pl
from jax.experimental.pallas import tpu as pltpu
from jax.sharding import Mesh, PartitionSpec as P

HQ = 32
HK = 4
DH = 128
GROUP = HQ // HK
ROWS = 64
QROWS = GROUP * ROWS
HALF = 2048
NBLK = 32
KB = 512
PER = KB // ROWS
PACK = 2 * ROWS + 16
PLANE = 16
CTX = ("zl", "y", "x")
NEG = -1e30
SCALE = 1.0 / math.sqrt(DH)
EXP_SCALE = SCALE * math.log2(math.e)
MIB = 1 << 20
bf16 = jnp.bfloat16
f32 = jnp.float32
i32 = jnp.int32


def dot(a, b):
    return lax.dot_general(a, b, (((1,), (0,)), ((), ())), preferred_element_type=f32)


def dot_tn(a, b):
    return lax.dot_general(a, b, (((0,), (0,)), ((), ())), preferred_element_type=f32)


def dot_nt(a, b):
    return lax.dot_general(a, b, (((1,), (1,)), ((), ())), preferred_element_type=f32)


def stack_heads(ref):
    return jnp.concatenate([ref[:, h * DH : (h + 1) * DH] for h in range(GROUP)], axis=0)


def where_am_i():
    side = lax.axis_index("resp")
    place = (lax.axis_index("zl") * 4 + lax.axis_index("y")) * 4 + lax.axis_index("x")
    return side, place


def start_copies(pairs, sems):
    copies = [pltpu.make_async_copy(s, d, sems.at[n]) for n, (s, d) in enumerate(pairs)]
    for c in copies:
        c.start()
    return copies


def key_pairs(ref, first, row, kp, vp):
    level = lax.axis_index("zl")
    pairs = []
    for n, z in enumerate((level, 1 - level)):
        to = pl.ds(first + z * PLANE, PLANE)
        pairs.append((ref.at[:, n, row : row + 64, :], kp.at[to]))
        pairs.append((ref.at[:, n, row + 64 : row + 128, :], vp.at[to]))
    return pairs


def prompt_pairs(side, own, other, kp, vp):
    return key_pairs(own, side * NBLK, 0, kp, vp) + key_pairs(other, (1 - side) * NBLK, 0, kp, vp)


def take(ref, first, rows):
    return ref[pl.ds(first, rows // ROWS), :, :].reshape(rows, DH)


def pick_start(doc, starts):
    low = jnp.where(doc >= 1, starts[0], 0)
    low = jnp.where(doc >= 2, starts[1], low)
    return jnp.where(doc >= 3, starts[2], low)


def key_positions(first, rows):
    return first + lax.broadcasted_iota(i32, (rows, QROWS), 0)


def lane_rows():
    return lax.broadcasted_iota(i32, (1, QROWS), 1) % ROWS


def head_lanes(row):
    return jnp.concatenate([row] * GROUP, axis=1)


def resp_range(resp_len, side, place):
    pos0 = place * ROWS
    live = resp_len[side]
    high = jnp.minimum(pos0 + lane_rows(), live - 1)
    blocks = jnp.minimum(pos0 + ROWS - 1, live - 1) // KB + 1
    return high, blocks


def pack_kernel(kp, vp, docs, kr, vr, out, ids, in_sems):
    copies = start_copies(
        [
            (docs, ids),
            (kp, out.at[0:64]),
            (vp, out.at[64:128]),
            (kr, out.at[PACK : PACK + 64]),
            (vr, out.at[PACK + 64 : PACK + 128]),
        ],
        in_sems,
    )
    copies[0].wait()
    row = jnp.concatenate([ids[...].astype(f32), jnp.full((1, DH - ROWS), 100.0, f32)], axis=1)
    out[128:144, :] = jnp.broadcast_to(row, (16, DH)).astype(bf16)
    for c in copies[1:]:
        c.wait()


def copies_kernel(own, other, prompt_out, resp_out, both, in_sems, sems):
    for c in start_copies([(own, both.at[0]), (other, both.at[1])], in_sems):
        c.wait()
    outs = [(both.at[:, 0:PACK, :], prompt_out.at[n]) for n in range(PLANE)]
    outs += [(both.at[:, PACK : PACK + 2 * ROWS, :], resp_out.at[n]) for n in range(PLANE)]
    for c in start_copies(outs, sems):
        c.wait()


def fwd_block(q_t, key, value, m_ref, l_ref, acc_ref, mask):
    z = dot(key, q_t) * EXP_SCALE
    if mask is not None:
        z = jnp.where(mask, z, NEG)
    old = m_ref[...]
    new = jnp.maximum(old, jnp.max(z, axis=0, keepdims=True))
    p = jnp.exp2(z - new)
    factor = jnp.exp2(old - new)
    m_ref[...] = new
    l_ref[...] = l_ref[...] * factor + jnp.sum(p, axis=0, keepdims=True)
    acc_ref[...] = acc_ref[...] * factor + dot_tn(value, p.astype(bf16))


def close_rows(m_ref, l_ref, acc_ref, att):
    total = l_ref[...]
    out = (acc_ref[...] / total).astype(bf16)
    rows = out.T
    for h in range(GROUP):
        att[:, h * DH : (h + 1) * DH] = rows[h * ROWS : (h + 1) * ROWS, :]
    return m_ref[...] + jnp.log2(total), out


def project(att, w_buf, tp, outs):
    all_att = att[...]
    width = outs[0].shape[1]
    for n, out in enumerate(outs):
        cols = pl.ds(pl.multiple_of(lax.rem(tp + n, 4) * width, width), width)
        out[...] = dot(all_att, w_buf[:, cols]).astype(bf16)


def row_deltas(d_t, out_t):
    return jnp.sum(d_t.astype(f32) * out_t.astype(f32), axis=0, keepdims=True)


def fwd_prompt_kernel(
    doc_ids, own, other, qp_in, qr_in, weight,
    out0, out1, out2, out3, out_t, stats, acc_out, win,
    kp, vp, docs, qp, qr, w_buf, att, m_ref, l_ref, acc_ref, sems, q_sems, w_sem,
):
    side, place = where_am_i()
    tp = lax.axis_index("tp")
    level = lax.axis_index("zl")
    q_copies = start_copies([(qp_in, qp), (qr_in, qr)], q_sems)
    pairs = prompt_pairs(side, own, other, kp, vp)
    for ref, first in ((own, side * NBLK), (other, (1 - side) * NBLK)):
        for n, z in enumerate((level, 1 - level)):
            pairs.append((ref.at[:, n, 128:144, :], docs.at[pl.ds(first + z * PLANE, PLANE)]))
    copies = start_copies(pairs, sems)
    w_copy = pltpu.make_async_copy(weight, w_buf, w_sem)
    w_copy.start()
    for c in q_copies:
        c.wait()
    q_t = stack_heads(qp).T
    r_t = stack_heads(qr).T
    for c in copies:
        c.wait()
    all_docs = docs[...].astype(f32).reshape(2 * NBLK * 16, DH)
    starts = []
    for n, value in enumerate((1.0, 2.0, 3.0)):
        count = jnp.sum(jnp.where(all_docs < value, 1.0 / 16, 0.0)).astype(i32)
        starts.append(count)

    def begin():
        m_ref[...] = jnp.full((1, QROWS), NEG, f32)
        l_ref[...] = jnp.zeros((1, QROWS), f32)
        acc_ref[...] = jnp.zeros((DH, QROWS), f32)

    begin()
    block = side * NBLK + place
    pos0 = block * ROWS
    low = pick_start(head_lanes(docs[block].astype(f32)[0:1, 0:ROWS]), starts)
    high = pos0 + lane_rows()
    low0 = pick_start(doc_ids[0], starts)
    win[0] = low0

    @pl.loop(low0 // KB, pos0 // KB + 1)
    def _(j):
        pos = key_positions(j * KB, KB)
        fwd_block(
            q_t, take(kp, j * PER, KB), take(vp, j * PER, KB), m_ref, l_ref, acc_ref,
            (pos >= low) & (pos <= high),
        )

    stats[0:1, :], out_t[...] = close_rows(m_ref, l_ref, acc_ref, att)
    begin()
    for j in range(4096 // KB):
        fwd_block(r_t, take(kp, j * PER, KB), take(vp, j * PER, KB), m_ref, l_ref, acc_ref, None)

    stats[1:2, :] = m_ref[...]
    stats[2:3, :] = l_ref[...]
    stats[4:5, :] = low.astype(f32)
    acc_out[...] = acc_ref[...]
    w_copy.wait()
    project(att, w_buf, tp, (out0, out1, out2, out3))

def resp_kernel(
    resp_len, own, qr_in, stats_in, acc_in, out_t_in, weight, *refs,
):
    cot_in = refs[:8]
    out0, out1, out2, out3, stats, g_resp, gq_ref, d_out = refs[8:16]
    kr, vr, qr, w_buf, cot, out_t_p, m_ref, l_ref, acc_ref, att, sems, c_sems, w_sem = refs[16:]
    side, place = where_am_i()
    tp = lax.axis_index("tp")
    copies = start_copies(
        key_pairs(own, 0, 0, kr, vr)
        + [(qr_in, qr), (stats_in, stats), (acc_in, acc_ref), (out_t_in, out_t_p)],
        sems,
    )
    w_copy = pltpu.make_async_copy(weight, w_buf, w_sem)
    w_copy.start()
    width = cot_in[0].shape[1]
    pairs = []
    for n, ref in enumerate(cot_in):
        cols = pl.ds(pl.multiple_of(lax.rem(tp + n // 2, 4) * width, width), width)
        pairs.append((ref, cot.at[pl.ds((n % 2) * ROWS, ROWS), cols]))
    c_copies = start_copies(pairs, c_sems)
    for c in copies:
        c.wait()
    q_rows = stack_heads(qr)
    q_t = q_rows.T
    m_ref[...] = stats[1:2, :]
    l_ref[...] = stats[2:3, :]
    high, used = resp_range(resp_len, side, place)

    @pl.loop(0, used)
    def _(j):
        pos = key_positions(j * KB, KB)
        fwd_block(
            q_t, take(kr, j * PER, KB), take(vr, j * PER, KB), m_ref, l_ref, acc_ref, pos <= high
        )

    log_total, out_t = close_rows(m_ref, l_ref, acc_ref, att)
    for c in c_copies:
        c.wait()
    w_copy.wait()
    d_all = dot(w_buf[...], cot[...].T).astype(bf16)
    for n in range(2):
        for h in range(GROUP):
            d_out[n, :, h * ROWS : (h + 1) * ROWS] = d_all[
                h * DH : (h + 1) * DH, n * ROWS : (n + 1) * ROWS
            ]
    d_t = d_out[1]
    d_rows = d_t.T
    delta = row_deltas(d_t, out_t)
    stats[1:2, :] = log_total
    stats[2:3, :] = row_deltas(d_out[0], out_t_p[...])
    stats[3:4, :] = delta
    gq_ref[...] = jnp.zeros((DH, QROWS), f32)

    @pl.loop(0, used)
    def _(j):
        pos = key_positions(j * KB, KB)
        g_key, g_value = bwd_block(
            q_t, q_rows, d_t, d_rows, take(kr, j * PER, KB), take(vr, j * PER, KB),
            log_total, delta, gq_ref, pos <= high,
        )
        blocks = pl.ds(j * PER, PER)
        g_resp[blocks, 0:64, :] = (g_key * SCALE).astype(bf16).reshape(PER, ROWS, DH)
        g_resp[blocks, 64:128, :] = g_value.astype(bf16).reshape(PER, ROWS, DH)

    @pl.loop(used, HALF // KB)
    def _(j):
        g_resp[pl.ds(j * PER, PER), :, :] = jnp.zeros((PER, 2 * ROWS, DH), bf16)

    project(att, w_buf, tp, (out0, out1, out2, out3))


def bwd_block(q_t, q_rows, d_t, d_rows, key, value, log_total, delta, gq_ref, mask):
    z = dot(key, q_t) * EXP_SCALE
    if mask is not None:
        z = jnp.where(mask, z, NEG)
    p = jnp.exp2(z - log_total)
    g_value = dot(p.astype(bf16), d_rows)
    dp = dot(value, d_t)
    ds = (p * (dp - delta)).astype(bf16)
    g_key = dot(ds, q_rows)
    gq_ref[...] += dot_tn(key, ds)
    return g_key, g_value


def store_q(gq_ref, out):
    rows = (gq_ref[...] * SCALE).astype(bf16).T
    for h in range(GROUP):
        out[:, h * DH : (h + 1) * DH] = rows[h * ROWS : (h + 1) * ROWS, :]


def bwd_prompt_kernel(
    win, own, other, qp_in, qr_in, d_in, stats_in, gq_in,
    gq_p, gq_r, g_mine, g_other,
    kp, vp, qp, qr, d_att, stats, gk, gv, gq_ref, sems,
):
    side, place = where_am_i()
    copies = start_copies(
        [(qr_in, qr), (qp_in, qp), (d_in, d_att), (stats_in, stats), (gq_in, gq_ref)]
        + prompt_pairs(side, own, other, kp, vp),
        sems,
    )
    for c in copies:
        c.wait()
    d_t = d_att[1]
    d_rows = d_t.T
    q_rows = stack_heads(qr)
    q_t = q_rows.T
    log_total = stats[1:2, :]
    delta = stats[3:4, :]

    @pl.loop(0, 4096 // KB // 4)
    def _(t):
        for u in range(4):
            j = t * 4 + u
            at = pl.ds(pl.multiple_of(j * KB, KB), KB)
            g_key, g_value = bwd_block(
                q_t, q_rows, d_t, d_rows, take(kp, j * PER, KB), take(vp, j * PER, KB),
                log_total, delta, gq_ref, None,
            )
            gk[at, :] = g_key
            gv[at, :] = g_value

    store_q(gq_ref, gq_r)

    d_t = d_att[0]
    d_rows = d_t.T
    q_rows = stack_heads(qp)
    q_t = q_rows.T
    log_total = stats[0:1, :]
    delta = stats[2:3, :]
    gq_ref[...] = jnp.zeros((DH, QROWS), f32)
    pos0 = (side * NBLK + place) * ROWS
    low = stats[4:5, :].astype(i32)
    high = pos0 + lane_rows()

    @pl.loop(win[0] // KB, pos0 // KB + 1)
    def _(j):
        at = pl.ds(pl.multiple_of(j * KB, KB), KB)
        pos = key_positions(j * KB, KB)
        g_key, g_value = bwd_block(
            q_t, q_rows, d_t, d_rows, take(kp, j * PER, KB), take(vp, j * PER, KB),
            log_total, delta, gq_ref, (pos >= low) & (pos <= high),
        )
        gk[at, :] += g_key
        gv[at, :] += g_value

    store_q(gq_ref, gq_p)

    @pl.loop(0, HALF // KB)
    def _(j):
        blocks = pl.ds(j * PER, PER)
        for base, out in ((side * HALF, g_mine), ((1 - side) * HALF, g_other)):
            at = pl.ds(pl.multiple_of(base + j * KB, KB), KB)
            out[blocks, 0:64, :] = (gk[at, :] * SCALE).astype(bf16).reshape(PER, ROWS, DH)
            out[blocks, 64:128, :] = gv[at, :].astype(bf16).reshape(PER, ROWS, DH)


def sum_kernel(prompt, resp, gk_p, gv_p, gk_r, gv_r):
    for ref, gk, gv in ((prompt, gk_p, gv_p), (resp, gk_r, gv_r)):
        total = ref[0].astype(f32)
        for n in range(1, NBLK):
            total = total + ref[n].astype(f32)
        gk[...] = total[0:64, :].astype(bf16)
        gv[...] = total[64:128, :].astype(bf16)


VM = pl.BlockSpec(memory_space=pltpu.VMEM)
SM = pl.BlockSpec(memory_space=pltpu.SMEM)
HB = pl.BlockSpec(memory_space=pltpu.HBM)


def shape(*dims, dtype=bf16):
    return jax.ShapeDtypeStruct(dims, dtype)


def call(kernel, name, in_specs, outs, scratch, args, gflop, out_specs=None, limit=58):
    return pl.pallas_call(
        kernel,
        out_shape=outs,
        in_specs=in_specs,
        out_specs=out_specs or (VM,) * len(outs),
        scratch_shapes=scratch,
        compiler_params=pltpu.CompilerParams(vmem_limit_bytes=limit * MIB),
        cost_estimate=pl.CostEstimate(
            flops=int(gflop * 1e9), bytes_accessed=4 * 10**6, transcendentals=10**6
        ),
        name=name,
    )(*args)


def state_scratch():
    return [pltpu.VMEM((1, QROWS), f32), pltpu.VMEM((1, QROWS), f32), pltpu.VMEM((DH, QROWS), f32)]


def key_scratch(blocks):
    return [pltpu.VMEM((blocks, ROWS, DH), bf16), pltpu.VMEM((blocks, ROWS, DH), bf16)]


def sems(n):
    return pltpu.SemaphoreType.DMA((n,))


SWAP = [(0, 1), (1, 0)]


def shift(x, by):
    return lax.ppermute(x, "tp", [(n, (n + by) % 4) for n in range(4)])


def add(*terms):
    total = terms[0].astype(f32)
    for t in terms[1:]:
        total = total + t.astype(f32)
    return total.astype(bf16)


def body(q_prompt, k_prompt, v_prompt, doc_ids, q_resp, k_resp, v_resp, resp_len, out_weight,
         grad_prompt, grad_resp):
    q_resp, k_resp, v_resp, grad_resp = q_resp[0], k_resp[0], v_resp[0], grad_resp[0]
    part = grad_prompt.shape[1]
    cols = GROUP * DH
    row_vm = pltpu.VMEM((ROWS, cols), bf16)
    weight_vm = pltpu.VMEM(out_weight.shape, bf16)
    stats_vm = pltpu.VMEM((8, QROWS), f32)

    left_p, left_r = shift(grad_prompt, 1), shift(grad_resp, 1)
    right_p, right_r = shift(grad_prompt, -1), shift(grad_resp, -1)
    (pack,) = call(
        pack_kernel, "pack_keys", [HB] * 5, (shape(PACK + 2 * ROWS, DH),),
        [pltpu.VMEM((1, ROWS), i32), sems(5)],
        (k_prompt, v_prompt, doc_ids.reshape(1, ROWS), k_resp, v_resp), 0.1,
    )
    pack_z = lax.ppermute(pack, "zl", SWAP)
    pack_p, pack_r = call(
        copies_kernel, "copy_packs", [HB] * 2,
        (shape(PLANE, 2, PACK, DH), shape(PLANE, 2, 2 * ROWS, DH)),
        [pltpu.VMEM((2, PACK + 2 * ROWS, DH), bf16), sems(2), sems(2 * PLANE)],
        (pack, pack_z), 0.1,
        out_specs=(HB, HB),
    )
    own_p = lax.all_to_all(pack_p, ("y", "x"), 0, 0, tiled=True)
    own_p, pack_r, left_p, left_r, right_p, right_r = lax.optimization_barrier(
        (own_p, pack_r, left_p, left_r, right_p, right_r)
    )
    far_p, far_r = shift(left_p, 1), shift(right_r, -1)
    own_r = lax.all_to_all(pack_r, ("y", "x"), 0, 0, tiled=True)
    other_p = lax.ppermute(own_p, "resp", SWAP)

    p0, p1, p2, p3, out_t, stats_p, acc_r, win = call(
        fwd_prompt_kernel, "forward_prompt_keys", [SM] + [HB] * 5,
        (shape(ROWS, part),) * 4
        + (
            shape(DH, QROWS), shape(8, QROWS, dtype=f32),
            shape(DH, QROWS, dtype=f32), shape(4, dtype=i32),
        ),
        key_scratch(2 * NBLK)
        + [pltpu.VMEM((2 * NBLK, 16, DH), bf16), row_vm, row_vm, weight_vm, row_vm]
        + state_scratch()
        + [sems(12), sems(2), pltpu.SemaphoreType.DMA(())],
        (doc_ids, own_p, other_p, q_prompt, q_resp, out_weight), 4,
        out_specs=(VM,) * 7 + (SM,),
    )
    out_p = add(p0, shift(p1, 1), shift(p2, 2), shift(p3, -1))

    r0, r1, r2, r3, stats, g_resp, gq_acc, d_att = call(
        resp_kernel, "response_keys", [SM] + [HB] * 14,
        (shape(ROWS, part),) * 4
        + (
            shape(8, QROWS, dtype=f32), shape(NBLK, 2 * ROWS, DH),
            shape(DH, QROWS, dtype=f32), shape(2, DH, QROWS),
        ),
        key_scratch(NBLK)
        + [
            row_vm, weight_vm, pltpu.VMEM((2 * ROWS, 4 * part), bf16),
            pltpu.VMEM((DH, QROWS), bf16),
        ]
        + state_scratch()
        + [row_vm, sems(8), sems(8), pltpu.SemaphoreType.DMA(())],
        (
            resp_len, own_r, q_resp, stats_p, acc_r, out_t, out_weight,
            grad_prompt, grad_resp, right_p, right_r, far_p, far_r, left_p, left_r,
        ), 4,
    )
    sums_r = lax.all_to_all(g_resp, CTX, 0, 0, tiled=True)
    gq_acc, out_p = lax.optimization_barrier((gq_acc, out_p))
    out_r = add(r0, shift(r1, 1), shift(r2, 2), shift(r3, -1))
    gq_p, gq_r, g_mine, g_other = call(
        bwd_prompt_kernel, "backward_prompt_keys", [SM] + [HB] * 7,
        (shape(ROWS, cols),) * 2 + (shape(NBLK, 2 * ROWS, DH),) * 2,
        key_scratch(2 * NBLK)
        + [
            row_vm, row_vm, pltpu.VMEM((2, DH, QROWS), bf16), stats_vm,
            pltpu.VMEM((4096, DH), f32), pltpu.VMEM((4096, DH), f32),
            pltpu.VMEM((DH, QROWS), f32), sems(13),
        ],
        (win, own_p, other_p, q_prompt, q_resp, d_att, stats, gq_acc), 8,
    )
    g_in = lax.ppermute(g_other, "resp", SWAP)
    g_in, out_r = lax.optimization_barrier((g_in, out_r))
    sums_p = lax.all_to_all(add(g_mine, g_in), CTX, 0, 0, tiled=True)
    gk_p, gv_p, gk_r, gv_r = call(
        sum_kernel, "sum_parts", [VM, VM], (shape(ROWS, DH),) * 4, [], (sums_p, sums_r), 0.1,
        limit=16,
    )
    return (out_p, out_r[None], gq_p, gk_p, gv_p, gq_r[None], gk_r[None], gv_r[None])


def solution(mesh):
    fine = Mesh(mesh.devices.reshape(2, 2, 4, 4, 4), ("resp", "zl", "y", "x", "tp"))
    rows = P(("resp",) + CTX, "tp")
    resp_rows = P("resp", CTX, "tp")
    in_specs = (
        rows, rows, rows, P(("resp",) + CTX), resp_rows, resp_rows, resp_rows, P(),
        P("tp", None), rows, resp_rows,
    )
    out_specs = (rows, resp_rows, rows, rows, rows, resp_rows, resp_rows, resp_rows)
    return jax.shard_map(body, mesh=fine, in_specs=in_specs, out_specs=out_specs, check_vma=False)
```

```python
import math

import jax
import jax.numpy as jnp
from jax import lax
from jax.experimental import pallas as pl
from jax.experimental.pallas import tpu as pltpu
from jax.sharding import Mesh, PartitionSpec as P

HQ = 32
HK = 4
DH = 128
GROUP = HQ // HK
ROWS = 64
QROWS = GROUP * ROWS
HALF = 2048
NBLK = 32
KB = 512
PER = KB // ROWS
PACK = 2 * ROWS + 16
PLANE = 16
CTX = ("zl", "y", "x")
NEG = -1e30
SCALE = 1.0 / math.sqrt(DH)
EXP_SCALE = SCALE * math.log2(math.e)
MIB = 1 << 20
bf16 = jnp.bfloat16
f32 = jnp.float32
i32 = jnp.int32


def dot(a, b):
    return lax.dot_general(a, b, (((1,), (0,)), ((), ())), preferred_element_type=f32)


def dot_tn(a, b):
    return lax.dot_general(a, b, (((0,), (0,)), ((), ())), preferred_element_type=f32)


def dot_nt(a, b):
    return lax.dot_general(a, b, (((1,), (1,)), ((), ())), preferred_element_type=f32)


def stack_heads(ref):
    return jnp.concatenate([ref[:, h * DH : (h + 1) * DH] for h in range(GROUP)], axis=0)


def where_am_i():
    side = lax.axis_index("resp")
    place = (lax.axis_index("zl") * 4 + lax.axis_index("y")) * 4 + lax.axis_index("x")
    return side, place


def start_copies(pairs, sems):
    copies = [pltpu.make_async_copy(s, d, sems.at[n]) for n, (s, d) in enumerate(pairs)]
    for c in copies:
        c.start()
    return copies


def key_pairs(ref, first, row, kp, vp):
    level = lax.axis_index("zl")
    pairs = []
    for n, z in enumerate((level, 1 - level)):
        to = pl.ds(first + z * PLANE, PLANE)
        pairs.append((ref.at[:, n, row : row + 64, :], kp.at[to]))
        pairs.append((ref.at[:, n, row + 64 : row + 128, :], vp.at[to]))
    return pairs


def take(ref, first, rows):
    return ref[pl.ds(first, rows // ROWS), :, :].reshape(rows, DH)


def pick_start(doc, starts):
    low = jnp.where(doc >= 1, starts[0], 0)
    low = jnp.where(doc >= 2, starts[1], low)
    return jnp.where(doc >= 3, starts[2], low)


def key_positions(first, rows):
    return first + lax.broadcasted_iota(i32, (rows, QROWS), 0)


def lane_rows():
    return lax.broadcasted_iota(i32, (1, QROWS), 1) % ROWS


def head_lanes(row):
    return jnp.concatenate([row] * GROUP, axis=1)


def resp_range(resp_len, side, place):
    pos0 = place * ROWS
    live = resp_len[side]
    high = jnp.minimum(pos0 + lane_rows(), live - 1)
    blocks = jnp.minimum(pos0 + ROWS - 1, live - 1) // KB + 1
    return high, blocks


def pack_kernel(kp, vp, docs, kr, vr, out, ids, in_sems):
    copies = start_copies(
        [
            (docs, ids),
            (kp, out.at[0:64]),
            (vp, out.at[64:128]),
            (kr, out.at[PACK : PACK + 64]),
            (vr, out.at[PACK + 64 : PACK + 128]),
        ],
        in_sems,
    )
    copies[0].wait()
    row = jnp.concatenate([ids[...].astype(f32), jnp.full((1, DH - ROWS), 100.0, f32)], axis=1)
    out[128:144, :] = jnp.broadcast_to(row, (16, DH)).astype(bf16)
    for c in copies[1:]:
        c.wait()


def copies_kernel(own, other, out, both, in_sems, sems):
    for c in start_copies([(own, both.at[0]), (other, both.at[1])], in_sems):
        c.wait()
    for c in start_copies([(both, out.at[n]) for n in range(PLANE)], sems):
        c.wait()


def cotangent_kernel(*refs):
    pieces, out, sems = refs[:8], refs[8], refs[9]
    tp = lax.axis_index("tp")
    width = pieces[0].shape[1]
    pairs = []
    for n, ref in enumerate(pieces):
        cols = pl.ds(pl.multiple_of(lax.rem(tp + n // 2, 4) * width, width), width)
        pairs.append((ref, out.at[pl.ds((n % 2) * ROWS, ROWS), cols]))
    for c in start_copies(pairs, sems):
        c.wait()


def fwd_block(q_t, key, value, m_ref, l_ref, acc_ref, mask):
    z = dot(key, q_t) * EXP_SCALE
    if mask is not None:
        z = jnp.where(mask, z, NEG)
    old = m_ref[...]
    new = jnp.maximum(old, jnp.max(z, axis=0, keepdims=True))
    p = jnp.exp2(z - new)
    factor = jnp.exp2(old - new)
    m_ref[...] = new
    l_ref[...] = l_ref[...] * factor + jnp.sum(p, axis=0, keepdims=True)
    acc_ref[...] = acc_ref[...] * factor + dot_tn(value, p.astype(bf16))


def close_rows(m_ref, l_ref, acc_ref, att):
    total = l_ref[...]
    out = (acc_ref[...] / total).astype(bf16)
    rows = out.T
    for h in range(GROUP):
        att[:, h * DH : (h + 1) * DH] = rows[h * ROWS : (h + 1) * ROWS, :]
    return m_ref[...] + jnp.log2(total), out


def project(att, w_buf, tp, outs):
    all_att = att[...]
    width = outs[0].shape[1]
    for n, out in enumerate(outs):
        cols = pl.ds(pl.multiple_of(lax.rem(tp + n, 4) * width, width), width)
        res = dot(all_att, w_buf[:, cols]).astype(bf16)
        if isinstance(out, tuple):
            out[0][...] = res[0:ROWS]
            out[1][...] = res[ROWS : 2 * ROWS]
        else:
            out[...] = res


def row_deltas(d_t, out_t):
    return jnp.sum(d_t.astype(f32) * out_t.astype(f32), axis=0, keepdims=True)


def forward_kernel(
    doc_ids, resp_len, own, other, qp_in, qr_in, weight, cot_in,
    out0, out1, out2p, out2r, out3, d_out, stats, win,
    kp, vp, kr, vr, docs, qp, qr, w_buf, cot, att, m_ref, l_ref, acc_ref,
    q_sems, sems, d_sems, r_sems, w_sem, c_sem,
):
    side, place = where_am_i()
    tp = lax.axis_index("tp")
    level = lax.axis_index("zl")
    q_copies = start_copies([(qp_in, qp), (qr_in, qr)], q_sems)
    pairs = []
    for ref, first in ((own, side * NBLK), (other, (1 - side) * NBLK)):
        for n, z in enumerate((level, 1 - level)):
            pairs.append((ref.at[:, n, 128:144, :], docs.at[pl.ds(first + z * PLANE, PLANE)]))
    d_copies = start_copies(pairs, d_sems)
    copies = start_copies(
        key_pairs(own, side * NBLK, 0, kp, vp) + key_pairs(other, (1 - side) * NBLK, 0, kp, vp),
        sems,
    )
    r_copies = start_copies(key_pairs(own, 0, PACK, kr, vr), r_sems)
    w_copy = pltpu.make_async_copy(weight, w_buf, w_sem)
    w_copy.start()
    c_copy = pltpu.make_async_copy(cot_in, cot, c_sem)
    c_copy.start()
    for c in q_copies:
        c.wait()
    q_t = stack_heads(qp).T
    r_t = stack_heads(qr).T
    for c in d_copies:
        c.wait()
    all_docs = docs[...].astype(f32).reshape(2 * NBLK * 16, DH)
    starts = []
    for value in (1.0, 2.0, 3.0):
        starts.append(jnp.sum(jnp.where(all_docs < value, 1.0 / 16, 0.0)).astype(i32))
    for c in copies:
        c.wait()

    def begin():
        m_ref[...] = jnp.full((1, QROWS), NEG, f32)
        l_ref[...] = jnp.zeros((1, QROWS), f32)
        acc_ref[...] = jnp.zeros((DH, QROWS), f32)

    begin()
    block = side * NBLK + place
    pos0 = block * ROWS
    low = pick_start(head_lanes(docs[block].astype(f32)[0:1, 0:ROWS]), starts)
    high = pos0 + lane_rows()
    low0 = pick_start(doc_ids[0], starts)
    win[0] = low0

    @pl.loop(low0 // KB, pos0 // KB + 1)
    def _(j):
        pos = key_positions(j * KB, KB)
        fwd_block(
            q_t, take(kp, j * PER, KB), take(vp, j * PER, KB), m_ref, l_ref, acc_ref,
            (pos >= low) & (pos <= high),
        )

    stats[0:1, :], out_p = close_rows(m_ref, l_ref, acc_ref, att.at[0:ROWS, :])
    c_copy.wait()
    w_copy.wait()
    d_all = dot(w_buf[...], cot[...].T).astype(bf16)
    for n in range(2):
        for h in range(GROUP):
            d_out[n, :, h * ROWS : (h + 1) * ROWS] = d_all[
                h * DH : (h + 1) * DH, n * ROWS : (n + 1) * ROWS
            ]
    stats[2:3, :] = row_deltas(d_out[0], out_p)
    begin()
    for j in range(4096 // KB):
        fwd_block(r_t, take(kp, j * PER, KB), take(vp, j * PER, KB), m_ref, l_ref, acc_ref, None)
    high, used = resp_range(resp_len, side, place)
    for c in r_copies:
        c.wait()

    @pl.loop(0, used)
    def _(j):
        pos = key_positions(j * KB, KB)
        fwd_block(
            r_t, take(kr, j * PER, KB), take(vr, j * PER, KB), m_ref, l_ref, acc_ref, pos <= high
        )

    stats[1:2, :], out_r = close_rows(m_ref, l_ref, acc_ref, att.at[ROWS : 2 * ROWS, :])
    stats[3:4, :] = row_deltas(d_out[1], out_r)
    stats[4:5, :] = low.astype(f32)
    project(att, w_buf, tp, (out0, out1, (out2p, out2r), out3))


def bwd_block(q_t, q_rows, d_t, d_rows, key, value, log_total, delta, gq_ref, mask):
    z = dot(key, q_t) * EXP_SCALE
    if mask is not None:
        z = jnp.where(mask, z, NEG)
    p = jnp.exp2(z - log_total)
    g_value = dot(p.astype(bf16), d_rows)
    dp = dot(value, d_t)
    ds = (p * (dp - delta)).astype(bf16)
    g_key = dot(ds, q_rows)
    gq_ref[...] += dot_tn(key, ds)
    return g_key, g_value


def store_q(gq_ref, out):
    rows = (gq_ref[...] * SCALE).astype(bf16).T
    for h in range(GROUP):
        out[:, h * DH : (h + 1) * DH] = rows[h * ROWS : (h + 1) * ROWS, :]


def query_side(q, d_att, stats, side):
    q_rows = stack_heads(q)
    d_t = d_att[side]
    return (q_rows.T, q_rows, d_t, d_t.T, stats[side : side + 1, :], stats[2 + side : 3 + side, :])


def store_keys(out, j, row, g_key, g_value):
    level = j * PER // PLANE
    n = jnp.abs(level - lax.axis_index("zl"))
    blocks = pl.ds(j * PER - level * PLANE, PER)
    out[blocks, n, row : row + 64, :] = (g_key * SCALE).astype(bf16).reshape(PER, ROWS, DH)
    out[blocks, n, row + 64 : row + 128, :] = g_value.astype(bf16).reshape(PER, ROWS, DH)


def half_of_prompt(base, first, pos0, low, kp, vp, gk, gv, prompt, resp, gqp_ref, gqr_ref, out):
    for j in range(HALF // KB):
        at = slice(j * KB, (j + 1) * KB)
        gk[at, :], gv[at, :] = bwd_block(
            *resp[:4], take(kp, j * PER, KB), take(vp, j * PER, KB), *resp[4:], gqr_ref, None
        )
    high = pos0 + lane_rows()
    last = jnp.minimum(pos0 // KB - base, HALF // KB - 1)

    @pl.loop(jnp.maximum(first // KB - base, 0), last + 1)
    def _(j):
        at = pl.ds(pl.multiple_of(j * KB, KB), KB)
        pos = key_positions((base + j) * KB, KB)
        g_key, g_value = bwd_block(
            *prompt[:4], take(kp, j * PER, KB), take(vp, j * PER, KB), *prompt[4:], gqp_ref,
            (pos >= low) & (pos <= high),
        )
        gk[at, :] += g_key
        gv[at, :] += g_value

    for j in range(HALF // KB):
        at = slice(j * KB, (j + 1) * KB)
        store_keys(out, j, 0, gk[at, :], gv[at, :])


def bwd_other_kernel(
    win, other, qp_in, qr_in, d_in, stats_in,
    g_out, gqp_ref, gqr_ref,
    kp, vp, qp, qr, d_att, stats, gk, gv, sems,
):
    side, place = where_am_i()
    copies = start_copies(
        [(qr_in, qr), (qp_in, qp), (d_in, d_att), (stats_in, stats)]
        + key_pairs(other, 0, 0, kp, vp),
        sems,
    )
    gqp_ref[...] = jnp.zeros((DH, QROWS), f32)
    gqr_ref[...] = jnp.zeros((DH, QROWS), f32)
    for c in copies:
        c.wait()
    half_of_prompt(
        (1 - side) * (HALF // KB), win[0], (side * NBLK + place) * ROWS, stats[4:5, :].astype(i32),
        kp, vp, gk, gv, query_side(qp, d_att, stats, 0), query_side(qr, d_att, stats, 1),
        gqp_ref, gqr_ref, g_out,
    )


def bwd_own_kernel(
    win, resp_len, own, qp_in, qr_in, d_in, stats_in, gqp_in, gqr_in,
    gq_p, gq_r, g_out,
    kp, vp, kr, vr, qp, qr, d_att, stats, gk, gv, gqp_ref, gqr_ref, sems, r_sems,
):
    side, place = where_am_i()
    copies = start_copies(
        [(qr_in, qr), (qp_in, qp), (d_in, d_att), (stats_in, stats)]
        + [(gqp_in, gqp_ref), (gqr_in, gqr_ref)]
        + key_pairs(own, 0, 0, kp, vp),
        sems,
    )
    r_copies = start_copies(key_pairs(own, 0, PACK, kr, vr), r_sems)
    for c in copies:
        c.wait()
    resp = query_side(qr, d_att, stats, 1)
    half_of_prompt(
        side * (HALF // KB), win[0], (side * NBLK + place) * ROWS, stats[4:5, :].astype(i32),
        kp, vp, gk, gv, query_side(qp, d_att, stats, 0), resp, gqp_ref, gqr_ref, g_out,
    )
    store_q(gqp_ref, gq_p)
    for c in r_copies:
        c.wait()
    high, used = resp_range(resp_len, side, place)

    @pl.loop(0, used)
    def _(j):
        pos = key_positions(j * KB, KB)
        g_key, g_value = bwd_block(
            *resp[:4], take(kr, j * PER, KB), take(vr, j * PER, KB), *resp[4:], gqr_ref, pos <= high
        )
        store_keys(g_out, j, 128, g_key, g_value)

    @pl.loop(used, HALF // KB)
    def _(j):
        zero = jnp.zeros((KB, DH), f32)
        store_keys(g_out, j, 128, zero, zero)

    store_q(gqr_ref, gq_r)


def sum_kernel(parts, mine, other):
    for n, out in ((0, mine), (1, other)):
        total = parts[0, n].astype(f32)
        for m in range(1, PLANE):
            total = total + parts[m, n].astype(f32)
        out[...] = total.astype(out.dtype)


def last_kernel(mine, other, gk_p, gv_p, gk_r, gv_r):
    total = mine[...] + other[...].astype(f32)
    for n, out in enumerate((gk_p, gv_p, gk_r, gv_r)):
        out[...] = total[n * ROWS : (n + 1) * ROWS, :].astype(bf16)


VM = pl.BlockSpec(memory_space=pltpu.VMEM)
SM = pl.BlockSpec(memory_space=pltpu.SMEM)
HB = pl.BlockSpec(memory_space=pltpu.HBM)
ANY = pl.BlockSpec(memory_space=pl.ANY)


def shape(*dims, dtype=bf16):
    return jax.ShapeDtypeStruct(dims, dtype)


def call(kernel, name, in_specs, outs, scratch, args, gflop, out_specs=None, limit=58):
    return pl.pallas_call(
        kernel,
        out_shape=outs,
        in_specs=in_specs,
        out_specs=out_specs or (VM,) * len(outs),
        scratch_shapes=scratch,
        compiler_params=pltpu.CompilerParams(vmem_limit_bytes=limit * MIB),
        cost_estimate=pl.CostEstimate(
            flops=int(gflop * 1e9), bytes_accessed=4 * 10**6, transcendentals=10**6
        ),
        name=name,
    )(*args)


def state_scratch():
    return [pltpu.VMEM((1, QROWS), f32), pltpu.VMEM((1, QROWS), f32), pltpu.VMEM((DH, QROWS), f32)]


def key_scratch(blocks):
    return [pltpu.VMEM((blocks, ROWS, DH), bf16), pltpu.VMEM((blocks, ROWS, DH), bf16)]


def sems(n):
    return pltpu.SemaphoreType.DMA((n,))


SWAP = [(0, 1), (1, 0)]


def shift(x, by):
    return lax.ppermute(x, "tp", [(n, (n + by) % 4) for n in range(4)])


def add(*terms):
    total = terms[0].astype(f32)
    for t in terms[1:]:
        total = total + t.astype(f32)
    return total.astype(bf16)


def body(q_prompt, k_prompt, v_prompt, doc_ids, q_resp, k_resp, v_resp, resp_len, out_weight,
         grad_prompt, grad_resp):
    q_resp, k_resp, v_resp, grad_resp = q_resp[0], k_resp[0], v_resp[0], grad_resp[0]
    part = grad_prompt.shape[1]
    cols = GROUP * DH
    row_vm = pltpu.VMEM((ROWS, cols), bf16)
    weight_vm = pltpu.VMEM(out_weight.shape, bf16)
    stats_vm = pltpu.VMEM((8, QROWS), f32)

    left_p, left_r = shift(grad_prompt, 1), shift(grad_resp, 1)
    right_p, right_r = shift(grad_prompt, -1), shift(grad_resp, -1)
    (pack,) = call(
        pack_kernel, "pack_keys", [HB] * 5, (shape(PACK + 2 * ROWS, DH),),
        [pltpu.VMEM((1, ROWS), i32), sems(5)],
        (k_prompt, v_prompt, doc_ids.reshape(1, ROWS), k_resp, v_resp), 0.1,
    )
    pack_z = lax.ppermute(pack, "zl", SWAP)
    (packs,) = call(
        copies_kernel, "copy_packs", [ANY] * 2, (shape(PLANE, 2, PACK + 2 * ROWS, DH),),
        [pltpu.VMEM((2, PACK + 2 * ROWS, DH), bf16), sems(2), sems(PLANE)],
        (pack, pack_z), 0.1, limit=16,
        out_specs=(HB,),
    )
    own = lax.all_to_all(packs, ("y", "x"), 0, 0, tiled=True)
    far_p, far_r = shift(left_p, 1), shift(right_r, -1)
    (cot,) = call(
        cotangent_kernel, "join_cotangent", [ANY] * 8, (shape(2 * ROWS, 4 * part),), [sems(8)],
        (grad_prompt, grad_resp, right_p, right_r, far_p, far_r, left_p, left_r), 0.1,
        out_specs=(HB,), limit=16,
    )
    own, cot = lax.optimization_barrier((own, cot))
    other = lax.ppermute(own[:, :, :PACK], "resp", SWAP)

    o0, o1, o2p, o2r, o3, d_att, stats, win = call(
        forward_kernel, "forward", [SM] * 2 + [ANY] * 2 + [HB] * 3 + [ANY],
        (
            shape(2 * ROWS, part), shape(2 * ROWS, part), shape(ROWS, part), shape(ROWS, part),
            shape(2 * ROWS, part), shape(2, DH, QROWS), shape(8, QROWS, dtype=f32),
            shape(4, dtype=i32),
        ),
        key_scratch(2 * NBLK)
        + key_scratch(NBLK)
        + [
            pltpu.VMEM((2 * NBLK, 16, DH), bf16), row_vm, row_vm, weight_vm,
            pltpu.VMEM((2 * ROWS, 4 * part), bf16), pltpu.VMEM((2 * ROWS, cols), bf16),
        ]
        + state_scratch()
        + [sems(2), sems(8), sems(4), sems(4)] + [pltpu.SemaphoreType.DMA(())] * 2,
        (
            doc_ids, resp_len, own, other, q_prompt, q_resp, out_weight, cot,
        ), 8,
        out_specs=(VM,) * 7 + (SM,), limit=40,
    )
    half_scratch = key_scratch(NBLK)
    side_scratch = [
        row_vm, row_vm, pltpu.VMEM((2, DH, QROWS), bf16), stats_vm,
        pltpu.VMEM((HALF, DH), f32), pltpu.VMEM((HALF, DH), f32),
    ]
    acc = shape(DH, QROWS, dtype=f32)
    g_other, gqp_acc, gqr_acc = call(
        bwd_other_kernel, "backward_other_half", [SM, ANY] + [HB] * 4,
        (shape(PLANE, 2, 2 * ROWS, DH), acc, acc),
        half_scratch + side_scratch + [sems(8)],
        (win, other, q_prompt, q_resp, d_att, stats), 4, limit=30,
    )
    g_in = lax.ppermute(g_other, "resp", SWAP)
    gq_p, gq_r, g_mine = call(
        bwd_own_kernel, "backward_own_half", [SM, SM, ANY] + [HB] * 6,
        (shape(ROWS, cols),) * 2 + (shape(PLANE, 2, 4 * ROWS, DH),),
        half_scratch + half_scratch + side_scratch
        + [pltpu.VMEM((DH, QROWS), f32)] * 2 + [sems(10), sems(4)],
        (win, resp_len, own, q_prompt, q_resp, d_att, stats, gqp_acc, gqr_acc), 7, limit=30,
    )
    sends = g_mine.at[:, :, : 2 * ROWS].set(add(g_mine[:, :, : 2 * ROWS], g_in))
    sends, o2p, o2r = lax.optimization_barrier((sends, o2p, o2r))
    parts = lax.all_to_all(sends, ("y", "x"), 0, 0, tiled=True)
    f_p, f_r = shift(o2p, 1), shift(o2r, -1)
    n1 = add(o1, jnp.pad(f_p, ((0, ROWS), (0, 0))))
    n3 = add(o3, jnp.pad(f_r, ((ROWS, 0), (0, 0))))
    left_out, right_out = shift(n1, 1), shift(n3, -1)
    out = add(o0, left_out, right_out)
    mine, other = call(
        sum_kernel, "sum_parts", [VM],
        (shape(4 * ROWS, DH, dtype=f32), shape(4 * ROWS, DH)), [], (parts,), 0.1, limit=16,
    )
    other = lax.ppermute(other, "zl", SWAP)
    gk_p, gv_p, gk_r, gv_r = call(
        last_kernel, "last_sum", [VM] * 2, (shape(ROWS, DH),) * 4, [], (mine, other), 0.1, limit=16,
    )
    return (out[:ROWS], out[ROWS:][None], gq_p, gk_p, gv_p, gq_r[None], gk_r[None], gv_r[None])


def solution(mesh):
    fine = Mesh(mesh.devices.reshape(2, 2, 4, 4, 4), ("resp", "zl", "y", "x", "tp"))
    rows = P(("resp",) + CTX, "tp")
    resp_rows = P("resp", CTX, "tp")
    in_specs = (
        rows, rows, rows, P(("resp",) + CTX), resp_rows, resp_rows, resp_rows, P(),
        P("tp", None), rows, resp_rows,
    )
    out_specs = (rows, resp_rows, rows, rows, rows, resp_rows, resp_rows, resp_rows)
    return jax.shard_map(body, mesh=fine, in_specs=in_specs, out_specs=out_specs, check_vma=False)
```

```python
import math

import jax
import jax.numpy as jnp
from jax import lax
from jax.experimental import pallas as pl
from jax.experimental.pallas import tpu as pltpu
from jax.sharding import Mesh, PartitionSpec as P

HQ = 32
HK = 4
DH = 128
GROUP = HQ // HK
ROWS = 64
QROWS = GROUP * ROWS
HALF = 2048
NBLK = 32
KB = 512
PER = KB // ROWS
WIN = 11
WKEYS = WIN * ROWS
LONG = 1024
PACK = 2 * ROWS + 16
PLANE = 16
CTX = ("zl", "y", "x")
NEG = -1e30
SCALE = 1.0 / math.sqrt(DH)
EXP_SCALE = SCALE * math.log2(math.e)
MIB = 1 << 20
bf16 = jnp.bfloat16
f32 = jnp.float32
i32 = jnp.int32


def dot(a, b):
    return lax.dot_general(a, b, (((1,), (0,)), ((), ())), preferred_element_type=f32)


def dot_tn(a, b):
    return lax.dot_general(a, b, (((0,), (0,)), ((), ())), preferred_element_type=f32)


def dot_nt(a, b):
    return lax.dot_general(a, b, (((1,), (1,)), ((), ())), preferred_element_type=f32)


def stack_heads(ref):
    return jnp.concatenate([ref[:, h * DH : (h + 1) * DH] for h in range(GROUP)], axis=0)


def where_am_i():
    side = lax.axis_index("resp")
    place = (lax.axis_index("zl") * 4 + lax.axis_index("y")) * 4 + lax.axis_index("x")
    return side, place


def start_copies(pairs, sems):
    copies = [pltpu.make_async_copy(s, d, sems.at[n]) for n, (s, d) in enumerate(pairs)]
    for c in copies:
        c.start()
    return copies


def key_pairs(ref, first, row, kp, vp):
    level = lax.axis_index("zl")
    pairs = []
    for n, z in enumerate((level, 1 - level)):
        to = pl.ds(first + z * PLANE, PLANE)
        pairs.append((ref.at[:, n, row : row + 64, :], kp.at[to]))
        pairs.append((ref.at[:, n, row + 64 : row + 128, :], vp.at[to]))
    return pairs


def take(ref, first, rows):
    return ref[pl.ds(first, rows // ROWS), :, :].reshape(rows, DH)


def pick_start(doc, starts):
    low = jnp.where(doc >= 1, starts[0], 0)
    low = jnp.where(doc >= 2, starts[1], low)
    return jnp.where(doc >= 3, starts[2], low)


def key_positions(first, rows):
    return first + lax.broadcasted_iota(i32, (rows, QROWS), 0)


def lane_rows():
    return lax.broadcasted_iota(i32, (1, QROWS), 1) % ROWS


def head_lanes(row):
    return jnp.concatenate([row] * GROUP, axis=1)


def resp_range(resp_len, side, place):
    pos0 = place * ROWS
    live = resp_len[side]
    high = jnp.minimum(pos0 + lane_rows(), live - 1)
    blocks = jnp.minimum(pos0 + ROWS - 1, live - 1) // LONG + 1
    return high, blocks


def pack_kernel(kp, vp, docs, kr, vr, out, ids, in_sems):
    copies = start_copies(
        [
            (docs, ids),
            (kp, out.at[0:64]),
            (vp, out.at[64:128]),
            (kr, out.at[PACK : PACK + 64]),
            (vr, out.at[PACK + 64 : PACK + 128]),
        ],
        in_sems,
    )
    copies[0].wait()
    row = jnp.concatenate([ids[...].astype(f32), jnp.full((1, DH - ROWS), 100.0, f32)], axis=1)
    out[128:144, :] = jnp.broadcast_to(row, (16, DH)).astype(bf16)
    for c in copies[1:]:
        c.wait()


def copies_kernel(own, other, out, both, in_sems, sems):
    for c in start_copies([(own, both.at[0]), (other, both.at[1])], in_sems):
        c.wait()
    for c in start_copies([(both, out.at[n]) for n in range(PLANE)], sems):
        c.wait()


def cotangent_kernel(*refs):
    pieces, out, sems = refs[:8], refs[8], refs[9]
    tp = lax.axis_index("tp")
    width = pieces[0].shape[1]
    pairs = []
    for n, ref in enumerate(pieces):
        cols = pl.ds(pl.multiple_of(lax.rem(tp + n // 2, 4) * width, width), width)
        pairs.append((ref, out.at[pl.ds((n % 2) * ROWS, ROWS), cols]))
    for c in start_copies(pairs, sems):
        c.wait()


def window(first, last, end):
    groups = jnp.maximum(last - first + WIN, 0) // WIN
    return groups, lambda t: (jnp.minimum(first + t * WIN, end - WIN), first + t * WIN)


def fwd_run(q_t, kp, vp, m_ref, l_ref, acc_ref):
    blocks = 4096 // KB
    m, l = m_ref[...], l_ref[...]
    z = dot(take(kp, 0, KB), q_t) * EXP_SCALE
    for j in range(blocks):
        ahead = dot(take(kp, (j + 1) * PER, KB), q_t) * EXP_SCALE if j + 1 < blocks else None
        new = jnp.maximum(m, jnp.max(z, axis=0, keepdims=True))
        p = jnp.exp2(z - new)
        factor = jnp.exp2(m - new)
        m = new
        l = l * factor + jnp.sum(p, axis=0, keepdims=True)
        acc_ref[...] = acc_ref[...] * factor + dot_tn(take(vp, j * PER, KB), p.astype(bf16))
        z = ahead
    m_ref[...] = m
    l_ref[...] = l


def fwd_block(q_t, key, value, m_ref, l_ref, acc_ref, mask):
    z = dot(key, q_t) * EXP_SCALE
    if mask is not None:
        z = jnp.where(mask, z, NEG)
    old = m_ref[...]
    new = jnp.maximum(old, jnp.max(z, axis=0, keepdims=True))
    p = jnp.exp2(z - new)
    factor = jnp.exp2(old - new)
    m_ref[...] = new
    l_ref[...] = l_ref[...] * factor + jnp.sum(p, axis=0, keepdims=True)
    acc_ref[...] = acc_ref[...] * factor + dot_tn(value, p.astype(bf16))


def close_rows(m_ref, l_ref, acc_ref, att):
    total = l_ref[...]
    out = (acc_ref[...] / total).astype(bf16)
    rows = out.T
    for h in range(GROUP):
        att[:, h * DH : (h + 1) * DH] = rows[h * ROWS : (h + 1) * ROWS, :]
    return m_ref[...] + jnp.log2(total), out


def project(att, w_buf, tp, outs):
    all_att = att[...]
    width = outs[0].shape[1]
    for n, out in enumerate(outs):
        cols = pl.ds(pl.multiple_of(lax.rem(tp + n, 4) * width, width), width)
        res = dot(all_att, w_buf[:, cols]).astype(bf16)
        if isinstance(out, tuple):
            out[0][...] = res[0:ROWS]
            out[1][...] = res[ROWS : 2 * ROWS]
        else:
            out[...] = res


def row_deltas(d_t, out_t):
    return jnp.sum(d_t.astype(f32) * out_t.astype(f32), axis=0, keepdims=True)


def forward_kernel(
    doc_ids, resp_len, own, other, qp_in, qr_in, weight, cot_in,
    out0, out1, out2p, out2r, out3, d_out, stats, win,
    kp, vp, kr, vr, docs, qp, qr, w_buf, cot, att, m_ref, l_ref, acc_ref,
    q_sems, sems, d_sems, r_sems, w_sem, c_sem,
):
    side, place = where_am_i()
    tp = lax.axis_index("tp")
    level = lax.axis_index("zl")
    q_copies = start_copies([(qp_in, qp), (qr_in, qr)], q_sems)
    pairs = []
    for ref, first in ((own, side * NBLK), (other, (1 - side) * NBLK)):
        for n, z in enumerate((level, 1 - level)):
            pairs.append((ref.at[:, n, 128:144, :], docs.at[pl.ds(first + z * PLANE, PLANE)]))
    d_copies = start_copies(pairs, d_sems)
    copies = start_copies(
        key_pairs(own, side * NBLK, 0, kp, vp) + key_pairs(other, (1 - side) * NBLK, 0, kp, vp),
        sems,
    )
    r_copies = start_copies(key_pairs(own, 0, PACK, kr, vr), r_sems)
    w_copy = pltpu.make_async_copy(weight, w_buf, w_sem)
    w_copy.start()
    c_copy = pltpu.make_async_copy(cot_in, cot, c_sem)
    c_copy.start()
    for c in q_copies:
        c.wait()
    q_t = stack_heads(qp).T
    r_t = stack_heads(qr).T
    for c in d_copies:
        c.wait()
    all_docs = docs[...].astype(f32).reshape(2 * NBLK * 16, DH)
    starts = []
    for value in (1.0, 2.0, 3.0):
        starts.append(jnp.sum(jnp.where(all_docs < value, 1.0 / 16, 0.0)).astype(i32))
    for c in copies:
        c.wait()

    def begin():
        m_ref[...] = jnp.full((1, QROWS), NEG, f32)
        l_ref[...] = jnp.zeros((1, QROWS), f32)
        acc_ref[...] = jnp.zeros((DH, QROWS), f32)

    begin()
    block = side * NBLK + place
    pos0 = block * ROWS
    low = pick_start(head_lanes(docs[block].astype(f32)[0:1, 0:ROWS]), starts)
    high = pos0 + lane_rows()
    low0 = pick_start(doc_ids[0], starts)
    win[0] = low0

    groups, group = window(low0 // ROWS, block, 2 * NBLK)

    @pl.loop(0, groups)
    def _(t):
        at, new = group(t)
        pos = key_positions(at * ROWS, WKEYS)
        fwd_block(
            q_t, take(kp, at, WKEYS), take(vp, at, WKEYS), m_ref, l_ref, acc_ref,
            (pos >= jnp.maximum(low, new * ROWS)) & (pos <= high),
        )

    stats[0:1, :], out_p = close_rows(m_ref, l_ref, acc_ref, att.at[0:ROWS, :])
    c_copy.wait()
    w_copy.wait()
    d_all = dot(w_buf[...], cot[...].T).astype(bf16)
    for n in range(2):
        for h in range(GROUP):
            d_out[n, :, h * ROWS : (h + 1) * ROWS] = d_all[
                h * DH : (h + 1) * DH, n * ROWS : (n + 1) * ROWS
            ]
    stats[2:3, :] = row_deltas(d_out[0], out_p)
    begin()
    fwd_run(r_t, kp, vp, m_ref, l_ref, acc_ref)
    high, used = resp_range(resp_len, side, place)
    for c in r_copies:
        c.wait()

    @pl.loop(0, used)
    def _(j):
        pos = key_positions(j * LONG, LONG)
        at = j * (LONG // ROWS)
        fwd_block(
            r_t, take(kr, at, LONG), take(vr, at, LONG), m_ref, l_ref, acc_ref, pos <= high
        )

    stats[1:2, :], out_r = close_rows(m_ref, l_ref, acc_ref, att.at[ROWS : 2 * ROWS, :])
    stats[3:4, :] = row_deltas(d_out[1], out_r)
    stats[4:5, :] = low.astype(f32)
    project(att, w_buf, tp, (out0, out1, (out2p, out2r), out3))


def bwd_scores(side, key, value):
    return dot(key, side[0]) * EXP_SCALE, dot(value, side[2])


def bwd_finish(side, key, z, dp, gq_ref):
    _, q_rows, _, d_rows, log_total, delta = side
    p = jnp.exp2(z - log_total)
    g_value = dot(p.astype(bf16), d_rows)
    ds = (p * (dp - delta)).astype(bf16)
    g_key = dot(ds, q_rows)
    gq_ref[...] += dot_tn(key, ds)
    return g_key, g_value


def bwd_block(side, key, value, gq_ref, mask):
    z, dp = bwd_scores(side, key, value)
    return bwd_finish(side, key, jnp.where(mask, z, NEG), dp, gq_ref)


def store_q(gq_ref, out):
    rows = (gq_ref[...] * SCALE).astype(bf16).T
    for h in range(GROUP):
        out[:, h * DH : (h + 1) * DH] = rows[h * ROWS : (h + 1) * ROWS, :]


def query_side(q, d_att, stats, side):
    q_rows = stack_heads(q)
    d_t = d_att[side]
    return (q_rows.T, q_rows, d_t, d_t.T, stats[side : side + 1, :], stats[2 + side : 3 + side, :])


def store_keys(out, j, row, g_key, g_value):
    blocks = g_key.shape[0] // ROWS
    level = j * blocks // PLANE
    n = jnp.abs(level - lax.axis_index("zl"))
    at = pl.ds(j * blocks - level * PLANE, blocks)
    out[at, n, row : row + 64, :] = (g_key * SCALE).astype(bf16).reshape(blocks, ROWS, DH)
    out[at, n, row + 64 : row + 128, :] = g_value.astype(bf16).reshape(blocks, ROWS, DH)


def half_of_prompt(base, first, block, low, kp, vp, gk, gv, prompt, resp, gqp_ref, gqr_ref, out):
    blocks = HALF // KB
    z, dp = bwd_scores(resp, take(kp, 0, KB), take(vp, 0, KB))
    for j in range(blocks):
        at = slice(j * KB, (j + 1) * KB)
        if j + 1 < blocks:
            ahead = bwd_scores(
                resp, take(kp, (j + 1) * PER, KB), take(vp, (j + 1) * PER, KB)
            )
        gk[at, :], gv[at, :] = bwd_finish(resp, take(kp, j * PER, KB), z, dp, gqr_ref)
        z, dp = ahead
    high = block * ROWS + lane_rows()
    groups, group = window(
        jnp.maximum(first // ROWS - base, 0), jnp.minimum(block - base, NBLK - 1), NBLK
    )

    @pl.loop(0, groups)
    def _(t):
        here, new = group(t)
        at = pl.ds(pl.multiple_of(here * ROWS, ROWS), WKEYS)
        pos = key_positions((base + here) * ROWS, WKEYS)
        g_key, g_value = bwd_block(
            prompt, take(kp, here, WKEYS), take(vp, here, WKEYS), gqp_ref,
            (pos >= jnp.maximum(low, (base + new) * ROWS)) & (pos <= high),
        )
        gk[at, :] += g_key
        gv[at, :] += g_value

    for j in range(HALF // KB):
        at = slice(j * KB, (j + 1) * KB)
        store_keys(out, j, 0, gk[at, :], gv[at, :])


def bwd_other_kernel(
    win, other, qp_in, qr_in, d_in, stats_in,
    g_out, gqp_ref, gqr_ref,
    kp, vp, qp, qr, d_att, stats, gk, gv, sems,
):
    side, place = where_am_i()
    copies = start_copies(
        [(qr_in, qr), (qp_in, qp), (d_in, d_att), (stats_in, stats)]
        + key_pairs(other, 0, 0, kp, vp),
        sems,
    )
    gqp_ref[...] = jnp.zeros((DH, QROWS), f32)
    gqr_ref[...] = jnp.zeros((DH, QROWS), f32)
    for c in copies:
        c.wait()
    half_of_prompt(
        (1 - side) * NBLK, win[0], side * NBLK + place, stats[4:5, :].astype(i32),
        kp, vp, gk, gv, query_side(qp, d_att, stats, 0), query_side(qr, d_att, stats, 1),
        gqp_ref, gqr_ref, g_out,
    )


def bwd_own_kernel(
    win, resp_len, own, qp_in, qr_in, d_in, stats_in, gqp_in, gqr_in,
    gq_p, gq_r, g_out,
    kp, vp, kr, vr, qp, qr, d_att, stats, gk, gv, gqp_ref, gqr_ref, sems, r_sems,
):
    side, place = where_am_i()
    copies = start_copies(
        [(qr_in, qr), (qp_in, qp), (d_in, d_att), (stats_in, stats)]
        + [(gqp_in, gqp_ref), (gqr_in, gqr_ref)]
        + key_pairs(own, 0, 0, kp, vp),
        sems,
    )
    r_copies = start_copies(key_pairs(own, 0, PACK, kr, vr), r_sems)
    for c in copies:
        c.wait()
    resp = query_side(qr, d_att, stats, 1)
    half_of_prompt(
        side * NBLK, win[0], side * NBLK + place, stats[4:5, :].astype(i32),
        kp, vp, gk, gv, query_side(qp, d_att, stats, 0), resp, gqp_ref, gqr_ref, g_out,
    )
    store_q(gqp_ref, gq_p)
    for c in r_copies:
        c.wait()
    high, used = resp_range(resp_len, side, place)

    @pl.loop(0, used)
    def _(j):
        pos = key_positions(j * LONG, LONG)
        at = j * (LONG // ROWS)
        g_key, g_value = bwd_block(
            resp, take(kr, at, LONG), take(vr, at, LONG), gqr_ref, pos <= high
        )
        store_keys(g_out, j, 128, g_key, g_value)

    @pl.loop(used, HALF // LONG)
    def _(j):
        zero = jnp.zeros((LONG, DH), f32)
        store_keys(g_out, j, 128, zero, zero)

    store_q(gqr_ref, gq_r)


def sum_kernel(parts, mine, other):
    for n, out in ((0, mine), (1, other)):
        total = parts[0, n].astype(f32)
        for m in range(1, PLANE):
            total = total + parts[m, n].astype(f32)
        out[...] = total.astype(out.dtype)


def last_kernel(mine, other, gk_p, gv_p, gk_r, gv_r):
    total = mine[...] + other[...].astype(f32)
    for n, out in enumerate((gk_p, gv_p, gk_r, gv_r)):
        out[...] = total[n * ROWS : (n + 1) * ROWS, :].astype(bf16)


VM = pl.BlockSpec(memory_space=pltpu.VMEM)
SM = pl.BlockSpec(memory_space=pltpu.SMEM)
HB = pl.BlockSpec(memory_space=pltpu.HBM)
ANY = pl.BlockSpec(memory_space=pl.ANY)


def shape(*dims, dtype=bf16):
    return jax.ShapeDtypeStruct(dims, dtype)


def call(kernel, name, in_specs, outs, scratch, args, gflop, out_specs=None, limit=58):
    return pl.pallas_call(
        kernel,
        out_shape=outs,
        in_specs=in_specs,
        out_specs=out_specs or (VM,) * len(outs),
        scratch_shapes=scratch,
        compiler_params=pltpu.CompilerParams(vmem_limit_bytes=limit * MIB),
        cost_estimate=pl.CostEstimate(
            flops=int(gflop * 1e9), bytes_accessed=4 * 10**6, transcendentals=10**6
        ),
        name=name,
    )(*args)


def state_scratch():
    return [pltpu.VMEM((1, QROWS), f32), pltpu.VMEM((1, QROWS), f32), pltpu.VMEM((DH, QROWS), f32)]


def key_scratch(blocks):
    return [pltpu.VMEM((blocks, ROWS, DH), bf16), pltpu.VMEM((blocks, ROWS, DH), bf16)]


def sems(n):
    return pltpu.SemaphoreType.DMA((n,))


SWAP = [(0, 1), (1, 0)]


def shift(x, by):
    return lax.ppermute(x, "tp", [(n, (n + by) % 4) for n in range(4)])


def add(*terms):
    total = terms[0].astype(f32)
    for t in terms[1:]:
        total = total + t.astype(f32)
    return total.astype(bf16)


def body(q_prompt, k_prompt, v_prompt, doc_ids, q_resp, k_resp, v_resp, resp_len, out_weight,
         grad_prompt, grad_resp):
    q_resp, k_resp, v_resp, grad_resp = q_resp[0], k_resp[0], v_resp[0], grad_resp[0]
    part = grad_prompt.shape[1]
    cols = GROUP * DH
    row_vm = pltpu.VMEM((ROWS, cols), bf16)
    weight_vm = pltpu.VMEM(out_weight.shape, bf16)
    stats_vm = pltpu.VMEM((8, QROWS), f32)

    left_p, left_r = shift(grad_prompt, 1), shift(grad_resp, 1)
    right_p, right_r = shift(grad_prompt, -1), shift(grad_resp, -1)
    (pack,) = call(
        pack_kernel, "pack_keys", [HB] * 5, (shape(PACK + 2 * ROWS, DH),),
        [pltpu.VMEM((1, ROWS), i32), sems(5)],
        (k_prompt, v_prompt, doc_ids.reshape(1, ROWS), k_resp, v_resp), 0.1,
    )
    pack_z = lax.ppermute(pack, "zl", SWAP)
    (packs,) = call(
        copies_kernel, "copy_packs", [ANY] * 2, (shape(PLANE, 2, PACK + 2 * ROWS, DH),),
        [pltpu.VMEM((2, PACK + 2 * ROWS, DH), bf16), sems(2), sems(PLANE)],
        (pack, pack_z), 0.1, limit=16,
        out_specs=(HB,),
    )
    own = lax.all_to_all(packs, ("y", "x"), 0, 0, tiled=True)
    far_p, far_r = shift(left_p, 1), shift(right_r, -1)
    (cot,) = call(
        cotangent_kernel, "join_cotangent", [ANY] * 8, (shape(2 * ROWS, 4 * part),), [sems(8)],
        (grad_prompt, grad_resp, right_p, right_r, far_p, far_r, left_p, left_r), 0.1,
        out_specs=(HB,), limit=16,
    )
    own, cot = lax.optimization_barrier((own, cot))
    other = lax.ppermute(own[:, :, :PACK], "resp", SWAP)

    o0, o1, o2p, o2r, o3, d_att, stats, win = call(
        forward_kernel, "forward", [SM] * 2 + [ANY] * 2 + [HB] * 3 + [ANY],
        (
            shape(2 * ROWS, part), shape(2 * ROWS, part), shape(ROWS, part), shape(ROWS, part),
            shape(2 * ROWS, part), shape(2, DH, QROWS), shape(8, QROWS, dtype=f32),
            shape(4, dtype=i32),
        ),
        key_scratch(2 * NBLK)
        + key_scratch(NBLK)
        + [
            pltpu.VMEM((2 * NBLK, 16, DH), bf16), row_vm, row_vm, weight_vm,
            pltpu.VMEM((2 * ROWS, 4 * part), bf16), pltpu.VMEM((2 * ROWS, cols), bf16),
        ]
        + state_scratch()
        + [sems(2), sems(8), sems(4), sems(4)] + [pltpu.SemaphoreType.DMA(())] * 2,
        (
            doc_ids, resp_len, own, other, q_prompt, q_resp, out_weight, cot,
        ), 8,
        out_specs=(VM,) * 7 + (SM,), limit=40,
    )
    half_scratch = key_scratch(NBLK)
    side_scratch = [
        row_vm, row_vm, pltpu.VMEM((2, DH, QROWS), bf16), stats_vm,
        pltpu.VMEM((HALF, DH), f32), pltpu.VMEM((HALF, DH), f32),
    ]
    acc = shape(DH, QROWS, dtype=f32)
    g_other, gqp_acc, gqr_acc = call(
        bwd_other_kernel, "backward_other_half", [SM, ANY] + [HB] * 4,
        (shape(PLANE, 2, 2 * ROWS, DH), acc, acc),
        half_scratch + side_scratch + [sems(8)],
        (win, other, q_prompt, q_resp, d_att, stats), 4, limit=30,
    )
    g_in = lax.ppermute(g_other, "resp", SWAP)
    gq_p, gq_r, g_mine = call(
        bwd_own_kernel, "backward_own_half", [SM, SM, ANY] + [HB] * 6,
        (shape(ROWS, cols),) * 2 + (shape(PLANE, 2, 4 * ROWS, DH),),
        half_scratch + half_scratch + side_scratch
        + [pltpu.VMEM((DH, QROWS), f32)] * 2 + [sems(10), sems(4)],
        (win, resp_len, own, q_prompt, q_resp, d_att, stats, gqp_acc, gqr_acc), 7, limit=30,
    )
    sends = g_mine.at[:, :, : 2 * ROWS].set(add(g_mine[:, :, : 2 * ROWS], g_in))
    sends, o2p, o2r = lax.optimization_barrier((sends, o2p, o2r))
    parts = lax.all_to_all(sends, ("y", "x"), 0, 0, tiled=True)
    f_p, f_r = shift(o2p, 1), shift(o2r, -1)
    n1 = add(o1, jnp.pad(f_p, ((0, ROWS), (0, 0))))
    n3 = add(o3, jnp.pad(f_r, ((ROWS, 0), (0, 0))))
    left_out, right_out = shift(n1, 1), shift(n3, -1)
    out = add(o0, left_out, right_out)
    mine, other = call(
        sum_kernel, "sum_parts", [VM],
        (shape(4 * ROWS, DH, dtype=f32), shape(4 * ROWS, DH)), [], (parts,), 0.1, limit=16,
    )
    other = lax.ppermute(other, "zl", SWAP)
    gk_p, gv_p, gk_r, gv_r = call(
        last_kernel, "last_sum", [VM] * 2, (shape(ROWS, DH),) * 4, [], (mine, other), 0.1, limit=16,
    )
    return (out[:ROWS], out[ROWS:][None], gq_p, gk_p, gv_p, gq_r[None], gk_r[None], gv_r[None])


def solution(mesh):
    fine = Mesh(mesh.devices.reshape(2, 2, 4, 4, 4), ("resp", "zl", "y", "x", "tp"))
    rows = P(("resp",) + CTX, "tp")
    resp_rows = P("resp", CTX, "tp")
    in_specs = (
        rows, rows, rows, P(("resp",) + CTX), resp_rows, resp_rows, resp_rows, P(),
        P("tp", None), rows, resp_rows,
    )
    out_specs = (rows, resp_rows, rows, rows, rows, resp_rows, resp_rows, resp_rows)
    return jax.shard_map(body, mesh=fine, in_specs=in_specs, out_specs=out_specs, check_vma=False)
```

```python
import math

import jax
import jax.numpy as jnp
from jax import lax
from jax.experimental import pallas as pl
from jax.experimental.pallas import tpu as pltpu
from jax.sharding import Mesh, PartitionSpec as P

HQ = 32
HK = 4
DH = 128
GROUP = HQ // HK
ROWS = 64
QROWS = GROUP * ROWS
HALF = 2048
NBLK = 32
KB = 512
PER = KB // ROWS
WIN = 11
WKEYS = WIN * ROWS
LONG = 1024
PACK = 2 * ROWS + 16
PLANE = 16
CTX = ("zl", "y", "x")
NEG = -1e30
SCALE = 1.0 / math.sqrt(DH)
EXP_SCALE = SCALE * math.log2(math.e)
MIB = 1 << 20
bf16 = jnp.bfloat16
f32 = jnp.float32
i32 = jnp.int32


def dot(a, b):
    return lax.dot_general(a, b, (((1,), (0,)), ((), ())), preferred_element_type=f32)


def dot_tn(a, b):
    return lax.dot_general(a, b, (((0,), (0,)), ((), ())), preferred_element_type=f32)


def dot_nt(a, b):
    return lax.dot_general(a, b, (((1,), (1,)), ((), ())), preferred_element_type=f32)


def stack_heads(ref):
    return jnp.concatenate([ref[:, h * DH : (h + 1) * DH] for h in range(GROUP)], axis=0)


def where_am_i():
    side = lax.axis_index("resp")
    place = (lax.axis_index("zl") * 4 + lax.axis_index("y")) * 4 + lax.axis_index("x")
    return side, place


def start_copies(pairs, sems):
    copies = [pltpu.make_async_copy(s, d, sems.at[n]) for n, (s, d) in enumerate(pairs)]
    for c in copies:
        c.start()
    return copies


def key_pairs(ref, first, row, kp, vp):
    level = lax.axis_index("zl")
    pairs = []
    for n, z in enumerate((level, 1 - level)):
        to = pl.ds(first + z * PLANE, PLANE)
        pairs.append((ref.at[:, n, row : row + 64, :], kp.at[to]))
        pairs.append((ref.at[:, n, row + 64 : row + 128, :], vp.at[to]))
    return pairs


def take(ref, first, rows):
    return ref[pl.ds(first, rows // ROWS), :, :].reshape(rows, DH)


def pick_start(doc, starts):
    low = jnp.where(doc >= 1, starts[0], 0)
    low = jnp.where(doc >= 2, starts[1], low)
    return jnp.where(doc >= 3, starts[2], low)


def key_positions(first, rows):
    return first + lax.broadcasted_iota(i32, (rows, QROWS), 0)


def lane_rows():
    return lax.broadcasted_iota(i32, (1, QROWS), 1) % ROWS


def head_lanes(row):
    return jnp.concatenate([row] * GROUP, axis=1)


def resp_range(resp_len, side, place):
    pos0 = place * ROWS
    live = resp_len[side]
    high = jnp.minimum(pos0 + lane_rows(), live - 1)
    blocks = jnp.minimum(pos0 + ROWS - 1, live - 1) // LONG + 1
    return high, blocks


def pack_kernel(kp, vp, docs, kr, vr, out, ids, in_sems):
    copies = start_copies(
        [
            (docs, ids),
            (kp, out.at[0:64]),
            (vp, out.at[64:128]),
            (kr, out.at[PACK : PACK + 64]),
            (vr, out.at[PACK + 64 : PACK + 128]),
        ],
        in_sems,
    )
    copies[0].wait()
    row = jnp.concatenate([ids[...].astype(f32), jnp.full((1, DH - ROWS), 100.0, f32)], axis=1)
    out[128:144, :] = jnp.broadcast_to(row, (16, DH)).astype(bf16)
    for c in copies[1:]:
        c.wait()


def copies_kernel(own, other, out, both, in_sems, sems):
    (copy,) = start_copies([(own, both.at[0])], in_sems)
    both[1] = other[...]
    copy.wait()
    for c in start_copies([(both, out.at[n]) for n in range(PLANE)], sems):
        c.wait()


def query_kernel(qp_in, qr_in, rows, turned, qp, qr, sems):
    copies = start_copies([(qp_in, qp), (qr_in, qr)], sems)
    for n, (ref, c) in enumerate(zip((qp, qr), copies)):
        c.wait()
        stacked = stack_heads(ref)
        rows[n] = stacked
        turned[n] = stacked.T


def cotangent_kernel(*refs):
    pieces, out, sems = refs[:8], refs[8], refs[9]
    tp = lax.axis_index("tp")
    width = pieces[0].shape[1]
    pairs = []
    for n, ref in enumerate(pieces):
        cols = pl.ds(pl.multiple_of(lax.rem(tp + n // 2, 4) * width, width), width)
        pairs.append((ref, out.at[pl.ds((n % 2) * ROWS, ROWS), cols]))
    for c in start_copies(pairs, sems):
        c.wait()


def window(first, last, end):
    groups = jnp.maximum(last - first + WIN, 0) // WIN
    return groups, lambda t: (jnp.minimum(first + t * WIN, end - WIN), first + t * WIN)


def fwd_run(q_t, kp, vp, m_ref, l_ref, acc_ref):
    blocks = 4096 // KB
    m, l = m_ref[...], l_ref[...]
    z = dot(take(kp, 0, KB), q_t) * EXP_SCALE
    for j in range(blocks):
        ahead = dot(take(kp, (j + 1) * PER, KB), q_t) * EXP_SCALE if j + 1 < blocks else None
        new = jnp.maximum(m, jnp.max(z, axis=0, keepdims=True))
        p = jnp.exp2(z - new)
        factor = jnp.exp2(m - new)
        m = new
        l = l * factor + jnp.sum(p, axis=0, keepdims=True)
        acc_ref[...] = acc_ref[...] * factor + dot_tn(take(vp, j * PER, KB), p.astype(bf16))
        z = ahead
    m_ref[...] = m
    l_ref[...] = l


def fwd_block(q_t, key, value, m_ref, l_ref, acc_ref, mask):
    z = dot(key, q_t) * EXP_SCALE
    if mask is not None:
        z = jnp.where(mask, z, NEG)
    old = m_ref[...]
    new = jnp.maximum(old, jnp.max(z, axis=0, keepdims=True))
    p = jnp.exp2(z - new)
    factor = jnp.exp2(old - new)
    m_ref[...] = new
    l_ref[...] = l_ref[...] * factor + jnp.sum(p, axis=0, keepdims=True)
    acc_ref[...] = acc_ref[...] * factor + dot_tn(value, p.astype(bf16))


def close_rows(m_ref, l_ref, acc_ref, att):
    total = l_ref[...]
    out = (acc_ref[...] / total).astype(bf16)
    rows = out.T
    for h in range(GROUP):
        att[:, h * DH : (h + 1) * DH] = rows[h * ROWS : (h + 1) * ROWS, :]
    return m_ref[...] + jnp.log2(total), out


def project(att, w_buf, tp, outs):
    all_att = att[...]
    width = outs[0].shape[1]
    for n, out in enumerate(outs):
        cols = pl.ds(pl.multiple_of(lax.rem(tp + n, 4) * width, width), width)
        res = dot(all_att, w_buf[:, cols]).astype(bf16)
        if isinstance(out, tuple):
            out[0][...] = res[0:ROWS]
            out[1][...] = res[ROWS : 2 * ROWS]
        else:
            out[...] = res


def row_deltas(d_t, out_t):
    return jnp.sum(d_t.astype(f32) * out_t.astype(f32), axis=0, keepdims=True)


def forward_kernel(
    doc_ids, resp_len, own, other, turned_in, weight, cot_in,
    out0, out1, out2p, out2r, out3, d_out, d_rows, stats, win,
    kp, vp, kr, vr, docs, turned, w_buf, cot, att, m_ref, l_ref, acc_ref,
    q_sems, sems, d_sems, r_sems, w_sem, c_sem,
):
    side, place = where_am_i()
    tp = lax.axis_index("tp")
    level = lax.axis_index("zl")
    (q_copy,) = start_copies([(turned_in, turned)], q_sems)
    pairs = []
    for ref, first in ((own, side * NBLK), (other, (1 - side) * NBLK)):
        for n, z in enumerate((level, 1 - level)):
            pairs.append((ref.at[:, n, 128:144, :], docs.at[pl.ds(first + z * PLANE, PLANE)]))
    d_copies = start_copies(pairs, d_sems)
    copies = start_copies(
        key_pairs(own, side * NBLK, 0, kp, vp) + key_pairs(other, (1 - side) * NBLK, 0, kp, vp),
        sems,
    )
    r_copies = start_copies(key_pairs(own, 0, PACK, kr, vr), r_sems)
    w_copy = pltpu.make_async_copy(weight, w_buf, w_sem)
    w_copy.start()
    c_copy = pltpu.make_async_copy(cot_in, cot, c_sem)
    c_copy.start()
    q_copy.wait()
    q_t = turned[0]
    r_t = turned[1]
    for c in d_copies:
        c.wait()
    all_docs = docs[...].astype(f32).reshape(2 * NBLK * 16, DH)
    starts = []
    for value in (1.0, 2.0, 3.0):
        starts.append(jnp.sum(jnp.where(all_docs < value, 1.0 / 16, 0.0)).astype(i32))
    for c in copies:
        c.wait()

    def begin():
        m_ref[...] = jnp.full((1, QROWS), NEG, f32)
        l_ref[...] = jnp.zeros((1, QROWS), f32)
        acc_ref[...] = jnp.zeros((DH, QROWS), f32)

    begin()
    block = side * NBLK + place
    pos0 = block * ROWS
    low = pick_start(head_lanes(docs[block].astype(f32)[0:1, 0:ROWS]), starts)
    high = pos0 + lane_rows()
    low0 = pick_start(doc_ids[0], starts)
    win[0] = low0

    groups, group = window(low0 // ROWS, block, 2 * NBLK)

    @pl.loop(0, groups)
    def _(t):
        at, new = group(t)
        pos = key_positions(at * ROWS, WKEYS)
        fwd_block(
            q_t, take(kp, at, WKEYS), take(vp, at, WKEYS), m_ref, l_ref, acc_ref,
            (pos >= jnp.maximum(low, new * ROWS)) & (pos <= high),
        )

    stats[0:1, :], out_p = close_rows(m_ref, l_ref, acc_ref, att.at[0:ROWS, :])
    c_copy.wait()
    w_copy.wait()
    d_all = dot(w_buf[...], cot[...].T).astype(bf16)
    for n in range(2):
        for h in range(GROUP):
            d_out[n, :, h * ROWS : (h + 1) * ROWS] = d_all[
                h * DH : (h + 1) * DH, n * ROWS : (n + 1) * ROWS
            ]
        d_rows[n] = d_out[n].T
    stats[2:3, :] = row_deltas(d_out[0], out_p)
    begin()
    fwd_run(r_t, kp, vp, m_ref, l_ref, acc_ref)
    high, used = resp_range(resp_len, side, place)
    for c in r_copies:
        c.wait()

    @pl.loop(0, used)
    def _(j):
        pos = key_positions(j * LONG, LONG)
        at = j * (LONG // ROWS)
        fwd_block(
            r_t, take(kr, at, LONG), take(vr, at, LONG), m_ref, l_ref, acc_ref, pos <= high
        )

    stats[1:2, :], out_r = close_rows(m_ref, l_ref, acc_ref, att.at[ROWS : 2 * ROWS, :])
    stats[3:4, :] = row_deltas(d_out[1], out_r)
    stats[4:5, :] = low.astype(f32)
    project(att, w_buf, tp, (out0, out1, (out2p, out2r), out3))


def bwd_scores(side, key, value):
    return dot(key, side[0]) * EXP_SCALE, dot(value, side[2])


def bwd_finish(side, key, z, dp, gq_ref):
    _, q_rows, _, d_rows, log_total, delta = side
    p = jnp.exp2(z - log_total)
    g_value = dot(p.astype(bf16), d_rows)
    ds = (p * (dp - delta)).astype(bf16)
    g_key = dot(ds, q_rows)
    gq_ref[...] += dot_tn(key, ds)
    return g_key, g_value


def bwd_block(side, key, value, gq_ref, mask):
    z, dp = bwd_scores(side, key, value)
    return bwd_finish(side, key, jnp.where(mask, z, NEG), dp, gq_ref)


def store_q(gq_ref, out):
    rows = (gq_ref[...] * SCALE).astype(bf16).T
    for h in range(GROUP):
        out[:, h * DH : (h + 1) * DH] = rows[h * ROWS : (h + 1) * ROWS, :]


def query_side(turned, rows, d_t, d_rows, stats, side):
    return (
        turned[side], rows[side], d_t[side], d_rows[side],
        stats[side : side + 1, :], stats[2 + side : 3 + side, :],
    )


def store_keys(out, j, row, g_key, g_value):
    blocks = g_key.shape[0] // ROWS
    level = j * blocks // PLANE
    n = jnp.abs(level - lax.axis_index("zl"))
    at = pl.ds(j * blocks - level * PLANE, blocks)
    out[at, n, row : row + 64, :] = (g_key * SCALE).astype(bf16).reshape(blocks, ROWS, DH)
    out[at, n, row + 64 : row + 128, :] = g_value.astype(bf16).reshape(blocks, ROWS, DH)


def half_of_prompt(base, first, block, low, kp, vp, gk, gv, prompt, resp, gqp_ref, gqr_ref, out):
    blocks = HALF // KB
    z, dp = bwd_scores(resp, take(kp, 0, KB), take(vp, 0, KB))
    for j in range(blocks):
        at = slice(j * KB, (j + 1) * KB)
        if j + 1 < blocks:
            ahead = bwd_scores(
                resp, take(kp, (j + 1) * PER, KB), take(vp, (j + 1) * PER, KB)
            )
        gk[at, :], gv[at, :] = bwd_finish(resp, take(kp, j * PER, KB), z, dp, gqr_ref)
        z, dp = ahead
    high = block * ROWS + lane_rows()
    groups, group = window(
        jnp.maximum(first // ROWS - base, 0), jnp.minimum(block - base, NBLK - 1), NBLK
    )

    @pl.loop(0, groups)
    def _(t):
        here, new = group(t)
        at = pl.ds(pl.multiple_of(here * ROWS, ROWS), WKEYS)
        pos = key_positions((base + here) * ROWS, WKEYS)
        g_key, g_value = bwd_block(
            prompt, take(kp, here, WKEYS), take(vp, here, WKEYS), gqp_ref,
            (pos >= jnp.maximum(low, (base + new) * ROWS)) & (pos <= high),
        )
        gk[at, :] += g_key
        gv[at, :] += g_value

    for j in range(HALF // KB):
        at = slice(j * KB, (j + 1) * KB)
        store_keys(out, j, 0, gk[at, :], gv[at, :])


def bwd_other_kernel(
    win, other, turned_in, rows_in, d_in, d_rows_in, stats_in,
    g_out, gqp_ref, gqr_ref,
    kp, vp, turned, rows, d_t, d_rows, stats, gk, gv, sems,
):
    side, place = where_am_i()
    copies = start_copies(
        [(turned_in, turned), (rows_in, rows), (d_in, d_t), (d_rows_in, d_rows)]
        + [(stats_in, stats)]
        + key_pairs(other, 0, 0, kp, vp),
        sems,
    )
    gqp_ref[...] = jnp.zeros((DH, QROWS), f32)
    gqr_ref[...] = jnp.zeros((DH, QROWS), f32)
    for c in copies:
        c.wait()
    half_of_prompt(
        (1 - side) * NBLK, win[0], side * NBLK + place, stats[4:5, :].astype(i32),
        kp, vp, gk, gv, query_side(turned, rows, d_t, d_rows, stats, 0),
        query_side(turned, rows, d_t, d_rows, stats, 1), gqp_ref, gqr_ref, g_out,
    )


def bwd_own_kernel(
    win, resp_len, own, turned_in, rows_in, d_in, d_rows_in, stats_in, gqp_in, gqr_in,
    gq_p, gq_r, g_out,
    kp, vp, kr, vr, turned, rows, d_t, d_rows, stats, gk, gv, gqp_ref, gqr_ref, sems, r_sems,
):
    side, place = where_am_i()
    copies = start_copies(
        [(turned_in, turned), (rows_in, rows), (d_in, d_t), (d_rows_in, d_rows)]
        + [(stats_in, stats), (gqp_in, gqp_ref), (gqr_in, gqr_ref)]
        + key_pairs(own, 0, 0, kp, vp),
        sems,
    )
    r_copies = start_copies(key_pairs(own, 0, PACK, kr, vr), r_sems)
    for c in copies:
        c.wait()
    resp = query_side(turned, rows, d_t, d_rows, stats, 1)
    half_of_prompt(
        side * NBLK, win[0], side * NBLK + place, stats[4:5, :].astype(i32),
        kp, vp, gk, gv, query_side(turned, rows, d_t, d_rows, stats, 0), resp,
        gqp_ref, gqr_ref, g_out,
    )
    store_q(gqp_ref, gq_p)
    for c in r_copies:
        c.wait()
    high, used = resp_range(resp_len, side, place)

    @pl.loop(0, used)
    def _(j):
        pos = key_positions(j * LONG, LONG)
        at = j * (LONG // ROWS)
        g_key, g_value = bwd_block(
            resp, take(kr, at, LONG), take(vr, at, LONG), gqr_ref, pos <= high
        )
        store_keys(g_out, j, 128, g_key, g_value)

    @pl.loop(used, HALF // LONG)
    def _(j):
        zero = jnp.zeros((LONG, DH), f32)
        store_keys(g_out, j, 128, zero, zero)

    store_q(gqr_ref, gq_r)


def sum_kernel(parts, mine, other):
    for n, out in ((0, mine), (1, other)):
        total = parts[0, n].astype(f32)
        for m in range(1, PLANE):
            total = total + parts[m, n].astype(f32)
        out[...] = total.astype(out.dtype)


def last_kernel(mine, other, gk_p, gv_p, gk_r, gv_r):
    total = mine[...] + other[...].astype(f32)
    for n, out in enumerate((gk_p, gv_p, gk_r, gv_r)):
        out[...] = total[n * ROWS : (n + 1) * ROWS, :].astype(bf16)


VM = pl.BlockSpec(memory_space=pltpu.VMEM)
SM = pl.BlockSpec(memory_space=pltpu.SMEM)
HB = pl.BlockSpec(memory_space=pltpu.HBM)
ANY = pl.BlockSpec(memory_space=pl.ANY)


def shape(*dims, dtype=bf16):
    return jax.ShapeDtypeStruct(dims, dtype)


def call(kernel, name, in_specs, outs, scratch, args, gflop, out_specs=None, limit=58):
    return pl.pallas_call(
        kernel,
        out_shape=outs,
        in_specs=in_specs,
        out_specs=out_specs or (VM,) * len(outs),
        scratch_shapes=scratch,
        compiler_params=pltpu.CompilerParams(vmem_limit_bytes=limit * MIB),
        cost_estimate=pl.CostEstimate(
            flops=int(gflop * 1e9), bytes_accessed=4 * 10**6, transcendentals=10**6
        ),
        name=name,
    )(*args)


def state_scratch():
    return [pltpu.VMEM((1, QROWS), f32), pltpu.VMEM((1, QROWS), f32), pltpu.VMEM((DH, QROWS), f32)]


def key_scratch(blocks):
    return [pltpu.VMEM((blocks, ROWS, DH), bf16), pltpu.VMEM((blocks, ROWS, DH), bf16)]


def sems(n):
    return pltpu.SemaphoreType.DMA((n,))


SWAP = [(0, 1), (1, 0)]


def shift(x, by):
    return lax.ppermute(x, "tp", [(n, (n + by) % 4) for n in range(4)])


def add(*terms):
    total = terms[0].astype(f32)
    for t in terms[1:]:
        total = total + t.astype(f32)
    return total.astype(bf16)


def body(q_prompt, k_prompt, v_prompt, doc_ids, q_resp, k_resp, v_resp, resp_len, out_weight,
         grad_prompt, grad_resp):
    q_resp, k_resp, v_resp, grad_resp = q_resp[0], k_resp[0], v_resp[0], grad_resp[0]
    part = grad_prompt.shape[1]
    cols = GROUP * DH
    row_vm = pltpu.VMEM((ROWS, cols), bf16)
    weight_vm = pltpu.VMEM(out_weight.shape, bf16)
    stats_vm = pltpu.VMEM((8, QROWS), f32)

    left_p, left_r = shift(grad_prompt, 1), shift(grad_resp, 1)
    right_p, right_r = shift(grad_prompt, -1), shift(grad_resp, -1)
    (pack,) = call(
        pack_kernel, "pack_keys", [HB] * 5, (shape(PACK + 2 * ROWS, DH),),
        [pltpu.VMEM((1, ROWS), i32), sems(5)],
        (k_prompt, v_prompt, doc_ids.reshape(1, ROWS), k_resp, v_resp), 0.1,
    )
    pack_z = lax.ppermute(pack, "zl", SWAP)
    (packs,) = call(
        copies_kernel, "copy_packs", [ANY, VM], (shape(PLANE, 2, PACK + 2 * ROWS, DH),),
        [pltpu.VMEM((2, PACK + 2 * ROWS, DH), bf16), sems(1), sems(PLANE)],
        (pack, pack_z), 0.1, limit=16,
        out_specs=(HB,),
    )
    own = lax.all_to_all(packs, ("y", "x"), 0, 0, tiled=True)
    far_p, far_r = shift(left_p, 1), shift(right_r, -1)
    q_rows, q_turned = call(
        query_kernel, "turn_queries", [HB] * 2, (shape(2, QROWS, DH), shape(2, DH, QROWS)),
        [row_vm, row_vm, sems(2)], (q_prompt, q_resp), 0.1,
    )
    (cot,) = call(
        cotangent_kernel, "join_cotangent", [ANY] * 8, (shape(2 * ROWS, 4 * part),), [sems(8)],
        (grad_prompt, grad_resp, right_p, right_r, far_p, far_r, left_p, left_r), 0.1,
        out_specs=(HB,), limit=16,
    )
    own, cot, q_rows, q_turned = lax.optimization_barrier((own, cot, q_rows, q_turned))
    other = lax.ppermute(own[:, :, :PACK], "resp", SWAP)

    o0, o1, o2p, o2r, o3, d_att, d_rows, stats, win = call(
        forward_kernel, "forward", [SM] * 2 + [ANY] * 3 + [HB] + [ANY],
        (
            shape(2 * ROWS, part), shape(2 * ROWS, part), shape(ROWS, part), shape(ROWS, part),
            shape(2 * ROWS, part), shape(2, DH, QROWS), shape(2, QROWS, DH),
            shape(8, QROWS, dtype=f32), shape(4, dtype=i32),
        ),
        key_scratch(2 * NBLK)
        + key_scratch(NBLK)
        + [
            pltpu.VMEM((2 * NBLK, 16, DH), bf16), pltpu.VMEM((2, DH, QROWS), bf16), weight_vm,
            pltpu.VMEM((2 * ROWS, 4 * part), bf16), pltpu.VMEM((2 * ROWS, cols), bf16),
        ]
        + state_scratch()
        + [sems(1), sems(8), sems(4), sems(4)] + [pltpu.SemaphoreType.DMA(())] * 2,
        (
            doc_ids, resp_len, own, other, q_turned, out_weight, cot,
        ), 8,
        out_specs=(VM,) * 8 + (SM,), limit=40,
    )
    half_scratch = key_scratch(NBLK)
    side_scratch = [
        pltpu.VMEM((2, DH, QROWS), bf16), pltpu.VMEM((2, QROWS, DH), bf16),
        pltpu.VMEM((2, DH, QROWS), bf16), pltpu.VMEM((2, QROWS, DH), bf16), stats_vm,
        pltpu.VMEM((HALF, DH), f32), pltpu.VMEM((HALF, DH), f32),
    ]
    acc = shape(DH, QROWS, dtype=f32)
    g_other, gqp_acc, gqr_acc = call(
        bwd_other_kernel, "backward_other_half", [SM] + [ANY] * 6,
        (shape(PLANE, 2, 2 * ROWS, DH), acc, acc),
        half_scratch + side_scratch + [sems(9)],
        (win, other, q_turned, q_rows, d_att, d_rows, stats), 4, limit=30,
    )
    g_in = lax.ppermute(g_other, "resp", SWAP)
    gq_p, gq_r, g_mine = call(
        bwd_own_kernel, "backward_own_half", [SM, SM] + [ANY] * 8,
        (shape(ROWS, cols),) * 2 + (shape(PLANE, 2, 4 * ROWS, DH),),
        half_scratch + half_scratch + side_scratch
        + [pltpu.VMEM((DH, QROWS), f32)] * 2 + [sems(11), sems(4)],
        (win, resp_len, own, q_turned, q_rows, d_att, d_rows, stats, gqp_acc, gqr_acc), 7, limit=30,
    )
    sends = g_mine.at[:, :, : 2 * ROWS].set(add(g_mine[:, :, : 2 * ROWS], g_in))
    sends, o2p, o2r = lax.optimization_barrier((sends, o2p, o2r))
    parts = lax.all_to_all(sends, ("y", "x"), 0, 0, tiled=True)
    f_p, f_r = shift(o2p, 1), shift(o2r, -1)
    n1 = add(o1, jnp.pad(f_p, ((0, ROWS), (0, 0))))
    n3 = add(o3, jnp.pad(f_r, ((ROWS, 0), (0, 0))))
    left_out, right_out = shift(n1, 1), shift(n3, -1)
    out = add(o0, left_out, right_out)
    mine, other = call(
        sum_kernel, "sum_parts", [VM],
        (shape(4 * ROWS, DH, dtype=f32), shape(4 * ROWS, DH)), [], (parts,), 0.1, limit=16,
    )
    other = lax.ppermute(other, "zl", SWAP)
    gk_p, gv_p, gk_r, gv_r = call(
        last_kernel, "last_sum", [VM] * 2, (shape(ROWS, DH),) * 4, [], (mine, other), 0.1, limit=16,
    )
    return (out[:ROWS], out[ROWS:][None], gq_p, gk_p, gv_p, gq_r[None], gk_r[None], gv_r[None])


def solution(mesh):
    fine = Mesh(mesh.devices.reshape(2, 2, 4, 4, 4), ("resp", "zl", "y", "x", "tp"))
    rows = P(("resp",) + CTX, "tp")
    resp_rows = P("resp", CTX, "tp")
    in_specs = (
        rows, rows, rows, P(("resp",) + CTX), resp_rows, resp_rows, resp_rows, P(),
        P("tp", None), rows, resp_rows,
    )
    out_specs = (rows, resp_rows, rows, rows, rows, resp_rows, resp_rows, resp_rows)
    return jax.shard_map(body, mesh=fine, in_specs=in_specs, out_specs=out_specs, check_vma=False)
```
